32 devices in a mesh: gx: 4 (over x, core), gy: 4 (over z), sec: 2 (over y).
Axes of the slice: x: 2, y: 2, z: 4, core: 2. Of those that a mesh axis runs over, the one named last changes fastest.
Arguments:
- pressure: float32 [32, 32, 256], P('gx', 'gy', 'sec'), may hold values from -6 to 6
- fluid_velocity: float32 [3, 32, 32, 256], P(None, 'gx', 'gy', 'sec'), may hold values from -6 to 6
- positions: float32 [3, 524288], P(None, ('gx', 'gy', 'sec')), may hold values from -24 to 24
- velocities: float32 [3, 524288], P(None, ('gx', 'gy', 'sec')), may hold values from -6 to 6
- volumes: float32 [524288], P(('gx', 'gy', 'sec')), may hold values from 0.05 to 0.4
- cells: int32 [524288], P(('gx', 'gy', 'sec')), may hold values from 0 to 16383
- partners: int32 [8, 524288], P(None, ('gx', 'gy', 'sec')), may hold values from 0 to 127
- departures: int32 [4, 32768], P(None, ('gx', 'gy', 'sec')), may hold values from 0 to 16383, as said below
Outputs:
- pressure_out: float32 [32, 32, 256], P('gx', 'gy', 'sec')
- velocity_out: float32 [3, 32, 32, 256], P(None, 'gx', 'gy', 'sec')
- positions_out: float32 [3, 524288], P(None, ('gx', 'gy', 'sec'))
- velocities_out: float32 [3, 524288], P(None, ('gx', 'gy', 'sec'))
The draws below stay inside these ranges and needn't reach their ends.
Inputs may be any that keep to these rules, and one draw needn't show every extreme that they name: Within each tile half's 1024 columns, the 4 x 1024 entries of departures are distinct particle indices of that tile half. cells[n] = x * 8 * 256 + y * 256 + z with x, y the cell's place within the tile and z its place along the whole depth.
All inputs are finite; a program needn't handle non-finite values.
Results may differ from the reference program's by a relative error of at most 0.00008.
Values sent between devices are 32-bit elements; how exact they have to be, the bound alone decides.
No kernel may reach another device: no remote copies, remote signals or barrier semaphores. Data moves between devices by JAX's collectives and lax.ppermute only.
A program may use at most 128 MiB of HBM per device.

```python
import math
import jax
import jax.numpy as jnp
from jax import lax

CX = 8
CY = 8
P_DEV = 16384
MOVERS = 1024
SWEEPS = 4
PAIRS = 8
BLOCK = 128
TILE_X = 4
TILE_Y = 4
HALVES = 2
TILES = 32
NX = 32
NY = 32
NZ = 256
PARTICLES = 524288


def draw_departures(key, part):
    tile_count = PARTICLES // P_DEV
    keys = jax.random.split(key, tile_count)
    chosen = jax.vmap(lambda single: jax.random.permutation(single, P_DEV)[:4 * MOVERS])(keys)
    chosen = chosen.reshape(tile_count, 4, MOVERS).transpose(1, 0, 2)
    return chosen.reshape(4, tile_count * MOVERS).astype(jnp.int32)


def touch_ends(drawn, own_key, smallest, high):
    index_at = [jax.random.randint(jax.random.fold_in(own_key, axis), (), 0, length) for axis, length in enumerate(drawn.shape)]
    main_axis = drawn.shape.index(max(drawn.shape))
    next_to = index_at[:main_axis] + [(index_at[main_axis] + 1) % drawn.shape[main_axis]] + index_at[main_axis + 1:]
    return drawn.at[tuple(index_at)].set(smallest).at[tuple(next_to)].set(high)


def levels(key, extent, pieces, low, largest):
    level, own = 1.0, jax.random.fold_in(key, 6)
    for dim, blocks in pieces:
        heights = jnp.exp(jax.random.uniform(jax.random.fold_in(own, dim), (blocks,), jnp.float32, low / len(pieces), largest / len(pieces)))
        level = level * jnp.repeat(heights, extent[dim] // blocks).reshape([-1 if axis == dim else 1 for axis in range(len(extent))])
    return level


def bell_draw(stream_key, shape, spread, reach, pieces=(), held_as=jnp.bfloat16):
    values = jax.random.normal(stream_key, shape, jnp.float32) * spread
    if len(pieces) > 0:
        values = levels(stream_key, shape, pieces, -0.22, 0.18) * values
    return jnp.clip(values, min=-reach, max=reach).astype(held_as)


def setup_inputs(seed: int = 0) -> dict:
    key_of = jax.random.split(jax.random.key(seed), 9)
    pressure = bell_draw(key_of[0], (NX, NY, NZ), 1.0, 6.0, ((0, 4), (1, 4), (2, 2)), jnp.float32)
    fluid_velocity = bell_draw(key_of[1], (3, NX, NY, NZ), 1.0, 6.0, ((1, 4), (2, 4), (3, 2)), jnp.float32)
    positions = bell_draw(key_of[2], (3, PARTICLES), 4.0, 24.0, ((1, 32),), jnp.float32)
    velocities = bell_draw(key_of[3], (3, PARTICLES), 1.0, 6.0, ((1, 32),), jnp.float32)
    volumes = jnp.clip(jnp.exp(math.log(0.4) - 2.0794415 * jax.random.uniform(key_of[4], (PARTICLES,), jnp.float32) ** levels(key_of[4], (PARTICLES,), ((0, 32),), -0.2, 0.2)), 0.05, 0.4)
    cells = touch_ends(jax.random.randint(key_of[5], (PARTICLES,), 0, CX * CY * NZ), jax.random.fold_in(key_of[5], 1), 0, (CX * CY * NZ) - 1).astype(jnp.int32)
    partners = touch_ends(jax.random.randint(key_of[6], (PAIRS, PARTICLES), 0, BLOCK), jax.random.fold_in(key_of[6], 1), 0, BLOCK - 1).astype(jnp.int32)
    departures = draw_departures(jax.random.fold_in(key_of[8], 71), 0)
    return dict(pressure=pressure, fluid_velocity=fluid_velocity, positions=positions, velocities=velocities, volumes=volumes, cells=cells, partners=partners, departures=departures)


TIME_STEP = 0.1
RELAX_RATE = 0.5
STIFFNESS = 1.0
DAMPING = 0.5
RANGE_SQUARED = 16.0
GRAVITY = 1.0


def contact_force(places, speeds, partner_rows):
    blocks = places.shape[1] // BLOCK
    place_b = places.reshape(3, blocks, BLOCK)
    speed_b = speeds.reshape(3, blocks, BLOCK)
    full_shape = (3, PAIRS, blocks, BLOCK)
    partner_index = jnp.broadcast_to(partner_rows.reshape(1, PAIRS, blocks, BLOCK), full_shape)
    other_place = jnp.take_along_axis(jnp.broadcast_to(place_b[:, None], full_shape), partner_index, axis=3)
    other_speed = jnp.take_along_axis(jnp.broadcast_to(speed_b[:, None], full_shape), partner_index, axis=3)
    separation = place_b[:, None] - other_place
    distance_sq = jnp.sum(separation * separation, axis=0)
    weight = 1.0 / (1.0 + distance_sq / RANGE_SQUARED)
    pushed = weight[None] * (STIFFNESS * separation + DAMPING * (other_speed - speed_b[:, None]))
    return jnp.sum(pushed, axis=1).reshape(3, -1)


def advance(places, speeds, volumes, void_at, flow_at, contact):
    drag_rate = RELAX_RATE * jnp.exp(-2.65 * jnp.log(void_at) - (2.0 / 3.0) * jnp.log(volumes))
    gravity_vec = jnp.array([-GRAVITY, 0.0, 0.0], dtype=jnp.float32)[:, None]
    moved_speed = (speeds + TIME_STEP * (drag_rate * flow_at + contact + gravity_vec)) / (1.0 + TIME_STEP * drag_rate)
    return places + TIME_STEP * moved_speed, moved_speed


def settle(tile_rows, chosen, arrived_a, arrived_b, arrived_c, arrived_d):
    tile_rows = tile_rows.at[:, chosen[1]].set(arrived_a)
    tile_rows = tile_rows.at[:, chosen[0]].set(arrived_b)
    tile_rows = tile_rows.at[:, chosen[3]].set(arrived_c)
    return tile_rows.at[:, chosen[2]].set(arrived_d)


def reference(pressure, fluid_velocity, positions, velocities, volumes, cells, partners, departures):
    tile_ids = jnp.arange(TILES, dtype=jnp.int32)
    owner_x = jnp.repeat(tile_ids // (TILE_Y * HALVES), P_DEV)
    owner_y = jnp.repeat((tile_ids // HALVES) % TILE_Y, P_DEV)
    global_cell = ((owner_x * CX + cells // (CY * NZ)) * NY + owner_y * CY + (cells // NZ) % CY) * NZ + cells % NZ
    solid = jax.ops.segment_sum(volumes, global_cell, num_segments=NX * NY * NZ).reshape(NX, NY, NZ)
    voidage = 1.0 / (1.0 + solid)
    face_coeffs = []
    diagonal = jnp.zeros_like(voidage)
    divergence = jnp.zeros_like(voidage)
    for direction in range(3):
        upper_face = 0.5 * (voidage + jnp.roll(voidage, -1, direction))
        lower_face = 0.5 * (voidage + jnp.roll(voidage, 1, direction))
        face_coeffs.append((upper_face, lower_face))
        diagonal = diagonal + upper_face + lower_face
        flux_part = voidage * fluid_velocity[direction]
        divergence = divergence + 0.5 * (jnp.roll(flux_part, -1, direction) - jnp.roll(flux_part, 1, direction))
    current = pressure
    for sweep_index in range(SWEEPS):
        neighbours = jnp.zeros_like(current)
        for direction in range(3):
            upper_face, lower_face = face_coeffs[direction]
            neighbours = neighbours + upper_face * jnp.roll(current, -1, direction) + lower_face * jnp.roll(current, 1, direction)
        current = (neighbours - divergence) / diagonal
    new_velocity = jnp.stack([fluid_velocity[direction] - 0.5 * (jnp.roll(current, -1, direction) - jnp.roll(current, 1, direction)) for direction in range(3)])
    void_at = voidage.reshape(-1)[global_cell]
    flow_at = new_velocity.reshape(3, -1)[:, global_cell]
    tile_places = positions.reshape(3, TILES, P_DEV).transpose(1, 0, 2)
    tile_speeds = velocities.reshape(3, TILES, P_DEV).transpose(1, 0, 2)
    tile_pairs = partners.reshape(PAIRS, TILES, P_DEV).transpose(1, 0, 2)
    contact = lax.map(lambda inputs: contact_force(inputs[0], inputs[1], inputs[2]), (tile_places, tile_speeds, tile_pairs))
    contact = contact.transpose(1, 0, 2).reshape(3, -1)
    moved_place, moved_speed = advance(positions, velocities, volumes, void_at, flow_at, contact)
    particle_state = jnp.concatenate([moved_place, moved_speed], axis=0).reshape(6, TILES, P_DEV).transpose(1, 0, 2)
    slot_lists = departures.reshape(4, TILES, MOVERS).transpose(1, 0, 2)
    leaving = jax.vmap(lambda tile_rows, chosen: tile_rows[:, chosen])(particle_state, slot_lists)
    leaving = leaving.reshape(TILE_X, TILE_Y, HALVES, 6, 4, MOVERS)
    arrived_a = jnp.roll(leaving[..., 0, :], 1, axis=0).reshape(TILES, 6, MOVERS)
    arrived_b = jnp.roll(leaving[..., 1, :], -1, axis=0).reshape(TILES, 6, MOVERS)
    arrived_c = jnp.roll(leaving[..., 2, :], 1, axis=1).reshape(TILES, 6, MOVERS)
    arrived_d = jnp.roll(leaving[..., 3, :], -1, axis=1).reshape(TILES, 6, MOVERS)
    settled = jax.vmap(settle)(particle_state, slot_lists, arrived_a, arrived_b, arrived_c, arrived_d)
    settled = settled.transpose(1, 0, 2).reshape(6, PARTICLES)
    return current, new_velocity, settled[:3], settled[3:]
```

```python
import functools

import jax
import jax.numpy as jnp
from jax import lax
from jax.experimental import pallas as pl
from jax.experimental.pallas import tpu as pltpu
from jax.sharding import PartitionSpec as P

SWEEPS = 4
PAIRS = 8
BLOCK = 128
LANES = 128
HALO = SWEEPS + 1

TIME_STEP = 0.1
RELAX_RATE = 0.5
DAMPING = 0.5
RANGE_SQUARED = 16.0
GRAVITY = 1.0

F32 = jnp.float32
BF16 = jnp.bfloat16
NT = (((1,), (1,)), ((), ()))


def call(kernel, outs, *args, scratch=(), flops=0, smem=()):
    outs_list = [jax.ShapeDtypeStruct(shape, dtype) for shape, dtype in outs]
    moved = sum(a.size * a.dtype.itemsize for a in list(args) + outs_list)
    vmem = pl.BlockSpec(memory_space=pltpu.VMEM)
    scalar = pl.BlockSpec(memory_space=pltpu.SMEM)
    return pl.pallas_call(
        kernel,
        out_shape=outs_list,
        in_specs=[scalar if i in smem else vmem for i in range(len(args))],
        out_specs=[vmem] * len(outs_list),
        scratch_shapes=list(scratch),
        compiler_params=pltpu.CompilerParams(vmem_limit_bytes=40 * 1024 * 1024),
        cost_estimate=pl.CostEstimate(flops=flops, bytes_accessed=moved, transcendentals=0),
    )(*args)


def split(values):
    high = values.astype(BF16)
    return high, (values - high.astype(F32)).astype(BF16)


def row16(row):
    return jnp.broadcast_to(row, (16, row.shape[1])).astype(BF16)


def counters():
    base = lax.broadcasted_iota(jnp.int32, (16, LANES), 0)
    return [(base + 16 * k).astype(F32).astype(BF16) for k in range(8)]


def one_hot(row, counts, values=None):
    wide = row16(row)
    zero = jnp.zeros((16, LANES), BF16)
    if values is None:
        values = jnp.ones((16, LANES), BF16)
    return jnp.concatenate([jnp.where(wide == c, values, zero) for c in counts], axis=0)


def cell_split(cells, sec):
    high = (cells >> 8) + 64 * (((cells >> 7) & 1) ^ sec)
    return high, cells & (LANES - 1)


def deposit_kernel(sec_ref, vol_ref, cell_ref, p_ref, v_ref, out_ref, hi_ref, lo_ref, va_ref, vb_ref):
    sec = sec_ref[0]
    high, low = cell_split(cell_ref[...], sec)
    hi_ref[...] = high.astype(F32)
    lo_ref[...] = low.astype(F32)
    vol = vol_ref[...]
    part = vol.astype(BF16).astype(F32)
    va_ref[...] = part
    vb_ref[...] = vol - part
    counts = counters()
    rows_each = 16
    steps = vol_ref.shape[0] // rows_each

    def step(i, acc):
        lefts, rights = [], []
        for r in range(rows_each):
            at = pl.ds(i * rows_each + r, 1)
            lefts.append(one_hot(hi_ref[at, :], counts))
            low_row = row16(lo_ref[at, :])
            zero = jnp.zeros((16, LANES), BF16)
            va, vb = row16(va_ref[at, :]), row16(vb_ref[at, :])
            hits = [low_row == c for c in counts]
            rights.append(
                jnp.concatenate(
                    [jnp.where(h, va, zero) for h in hits] + [jnp.where(h, vb, zero) for h in hits],
                    axis=0,
                )
            )
        left = jnp.concatenate(lefts, axis=1)
        right = jnp.concatenate(rights, axis=1)
        return acc + lax.dot_general(left, right, NT, preferred_element_type=F32)

    acc = lax.fori_loop(0, steps, step, jnp.zeros((LANES, 2 * LANES), F32))
    out_ref[0:128, :] = acc[:, :LANES] + acc[:, LANES:]
    out_ref[128:192, :] = p_ref[...].reshape(64, LANES)
    out_ref[192:384, :] = v_ref[...].reshape(192, LANES)


def contact_kernel(vol_ref, pos_ref, vel_ref, pair_ref, base_ref):
    blocks = pos_ref.shape[1] // BLOCK
    base_ref[6] = RELAX_RATE * jnp.exp((-2.0 / 3.0) * jnp.log(vol_ref[...]))

    def step(b, carry):
        at = pl.ds(pl.multiple_of(b * BLOCK, BLOCK), BLOCK)
        index = pair_ref[:, at]
        mine = [pos_ref[d : d + 1, at] for d in range(3)] + [vel_ref[d : d + 1, at] for d in range(3)]
        wide = [jnp.broadcast_to(m, (PAIRS, BLOCK)) for m in mine]
        other = [jnp.take_along_axis(w, index, axis=1, mode="promise_in_bounds") for w in wide]
        apart = [wide[d] - other[d] for d in range(3)]
        dist = apart[0] * apart[0] + apart[1] * apart[1] + apart[2] * apart[2]
        weight = 1.0 / (1.0 + dist * (1.0 / RANGE_SQUARED))
        for d in range(3):
            push = weight * (apart[d] + DAMPING * (other[3 + d] - wide[3 + d]))
            force = jnp.sum(push, axis=0, keepdims=True)
            if d == 0:
                force = force - GRAVITY
            base_ref[d, pl.ds(b, 1), :] = mine[d]
            base_ref[3 + d, pl.ds(b, 1), :] = mine[3 + d] + TIME_STEP * force
        return carry

    lax.fori_loop(0, blocks, step, 0, unroll=4)


def table_of(fields, table_ref):
    for f, values in enumerate(fields):
        high, low = split(jnp.swapaxes(values, 0, 1))
        table_ref[f * LANES : (f + 1) * LANES, :LANES] = high
        table_ref[f * LANES : (f + 1) * LANES, LANES:] = low


def pick(table_ref, fields, high_rows, low_rows, counts):
    hot = jnp.concatenate([one_hot(row, counts) for row in high_rows], axis=1)
    hot = jnp.concatenate([hot, hot], axis=0)
    lane = lax.broadcasted_iota(jnp.int32, (LANES, LANES), 0).astype(F32)
    hits = [jnp.broadcast_to(row, (LANES, LANES)) == lane for row in low_rows]
    found = []
    for f in range(fields):
        rows = jnp.dot(table_ref[f * LANES : (f + 1) * LANES, :], hot, preferred_element_type=F32)
        found.append(
            [
                jnp.sum(jnp.where(hit, rows[:, LANES * h : LANES * (h + 1)], 0.0), axis=0, keepdims=True)
                for h, hit in enumerate(hits)
            ]
        )
    return found


def leave_kernel(sec_ref, base_ref, cell_ref, dep_ref, out_ref, mask_ref, hi_ref, lo_ref, table_ref):
    sec = sec_ref[0]
    high, low = cell_split(cell_ref[...], sec)
    cell = (high * LANES + low).astype(F32)
    table_of([base_ref[f] for f in range(7)] + [cell], table_ref)
    dep = dep_ref[...]
    hi_ref[...] = (dep >> 7).astype(F32)
    lo_ref[...] = (dep & (LANES - 1)).astype(F32)
    counts = counters()
    mask = jnp.zeros((LANES, LANES), F32)
    movers = dep_ref.shape[1]
    for r in range(4):

        def step(i, mask):
            ats = [pl.ds(pl.multiple_of(i * 256 + 128 * h, 128), 128) for h in range(2)]
            his = [hi_ref[r : r + 1, at] for at in ats]
            los = [lo_ref[r : r + 1, at] for at in ats]
            found = pick(table_ref, 8, his, los, counts)
            for f in range(8):
                for h in range(2):
                    out_ref[f, pl.ds(r * (movers // LANES) + i * 2 + h, 1), :] = found[f][h]
            left = jnp.concatenate([one_hot(row, counts) for row in his], axis=1)
            right = jnp.concatenate([one_hot(row, counts) for row in los], axis=1)
            return mask + lax.dot_general(left, right, NT, preferred_element_type=F32)

        mask = lax.fori_loop(0, movers // 256, step, mask)
    mask_ref[...] = mask


def tile_kernel(mine_ref, got_ref, tile_ref, up_ref, down_ref):
    own = mine_ref[0:64, :] + got_ref[64:128, :]
    far = mine_ref[64:128, :] + got_ref[0:64, :]
    tile_ref[0] = 1.0 / (1.0 + own)
    tile_ref[1] = 1.0 / (1.0 + far)
    for f in range(4):
        tile_ref[2 + 2 * f] = mine_ref[128 + 64 * f : 192 + 64 * f, :]
        tile_ref[3 + 2 * f] = got_ref[128 + 64 * f : 192 + 64 * f, :]
    for g in range(10):
        for j in range(HALO):
            up_ref[g, 8 * j : 8 * j + 8, :] = tile_ref[g, pl.ds(8 - HALO + j, 8, stride=8), :]
            down_ref[g, 8 * j : 8 * j + 8, :] = tile_ref[g, pl.ds(j, 8, stride=8), :]


def side_kernel(tile_ref, low_ref, high_ref, up_ref, down_ref):
    for g in range(10):
        for x in range(8):
            slab = jnp.concatenate(
                [
                    low_ref[g, pl.ds(8 + x, 4, stride=8), :],
                    tile_ref[g, 8 * x : 8 * x + 8, :],
                    high_ref[g, pl.ds(x, 4, stride=8), :],
                ],
                axis=0,
            )
            if x >= 8 - HALO:
                at = x - (8 - HALO)
                up_ref[g, 16 * at : 16 * at + 16, :] = slab
            if x < HALO:
                down_ref[g, 16 * x : 16 * x + 16, :] = slab


def fluid_kernel(
    tile_ref, ylow_ref, yhigh_ref, xlow_ref, xhigh_ref, leave_ref,
    p_out_ref, v_out_ref, table_ref, sent_ref,
    grid_ref, other_ref, invd_ref, div_ref, face_ref,
):
    size = 8 + 2 * HALO
    for f in range(5):
        for h in range(2):
            g = 2 * f + h
            lanes = slice(LANES * h, LANES * (h + 1))
            for j in range(HALO):
                grid_ref[f, j, 0:16, lanes] = xlow_ref[g, 16 * j : 16 * j + 16, :]
                grid_ref[f, j, 16:24, lanes] = jnp.ones((8, LANES), F32)
                grid_ref[f, 8 + HALO + j, 0:16, lanes] = xhigh_ref[g, 16 * j : 16 * j + 16, :]
                grid_ref[f, 8 + HALO + j, 16:24, lanes] = jnp.ones((8, LANES), F32)
            for x in range(8):
                grid_ref[f, HALO + x, 0:24, lanes] = jnp.concatenate(
                    [
                        ylow_ref[g, pl.ds(8 + x, 4, stride=8), :],
                        tile_ref[g, 8 * x : 8 * x + 8, :],
                        yhigh_ref[g, pl.ds(x, 5, stride=8), :],
                        jnp.ones((6, LANES), F32),
                        ylow_ref[g, x : x + 1, :],
                    ],
                    axis=0,
                )

    def around(values):
        return (
            pltpu.roll(values, 23, 0),
            pltpu.roll(values, 1, 0),
            pltpu.roll(values, 255, 1),
            pltpu.roll(values, 1, 1),
        )

    def setup(x, carry):
        void = grid_ref[0, x]
        above, below = grid_ref[0, x + 1], grid_ref[0, x - 1]
        sides = around(void)
        total = 6.0 * void + above + below
        for k in range(4):
            total = total + sides[k]
            face_ref[k, x] = void + sides[k]
        invd_ref[x] = 1.0 / total
        ys = around(void * grid_ref[3, x])
        zs = around(void * grid_ref[4, x])
        div_ref[x] = (
            above * grid_ref[2, x + 1] - below * grid_ref[2, x - 1] + ys[0] - ys[1] + zs[2] - zs[3]
        )
        return carry

    lax.fori_loop(1, size - 1, setup, 0)

    for t in range(SWEEPS):
        source = grid_ref.at[1] if t % 2 == 0 else other_ref
        target = other_ref if t % 2 == 0 else grid_ref.at[1]

        def sweep(x, carry):
            void = grid_ref[0, x]
            sides = around(source[x])
            total = (void + grid_ref[0, x + 1]) * source[x + 1] - div_ref[x]
            total = total + (void + grid_ref[0, x - 1]) * source[x - 1]
            for k in range(4):
                total = total + face_ref[k, x] * sides[k]
            target[x] = total * invd_ref[x]
            return carry

        lax.fori_loop(1 + t, size - 1 - t, sweep, 0)

    final = grid_ref.at[1]
    tables = [[], [], [], []]
    for x in range(8):
        values = final[HALO + x]
        sides = around(values)
        flows = (
            grid_ref[2, HALO + x] - 0.5 * (final[HALO + x + 1] - final[HALO + x - 1]),
            grid_ref[3, HALO + x] - 0.5 * (sides[0] - sides[1]),
            grid_ref[4, HALO + x] - 0.5 * (sides[2] - sides[3]),
        )
        p_out_ref[x] = values[4:12, :LANES]
        drag = jnp.exp(-2.65 * jnp.log(grid_ref[0, HALO + x]))[4:12]
        tables[0].append(drag)
        for d in range(3):
            kept = flows[d][4:12]
            v_out_ref[d, x] = kept[:, :LANES]
            tables[1 + d].append(kept)
    fields = []
    for f in range(4):
        whole = jnp.concatenate(tables[f], axis=0)
        fields.append(jnp.concatenate([whole[:, :LANES], whole[:, LANES:]], axis=0))
    table_of(fields, table_ref)

    counts = counters()
    count = leave_ref.shape[1]

    def step(i, carry):
        his, los = [], []
        for h in range(2):
            cell = leave_ref[7, pl.ds(2 * i + h, 1), :].astype(jnp.int32)
            his.append((cell >> 7).astype(F32))
            los.append((cell & (LANES - 1)).astype(F32))
        found = pick(table_ref, 4, his, los, counts)
        for f in range(4):
            for h in range(2):
                sent_ref[f, pl.ds(2 * i + h, 1), :] = found[f][h]
        return carry

    lax.fori_loop(0, count // 2, step, 0)
    drag = TIME_STEP * sent_ref[0] * leave_ref[6]
    scale = 1.0 / (1.0 + drag)
    speeds = [(leave_ref[3 + d] + drag * sent_ref[1 + d]) * scale for d in range(3)]
    for d in range(3):
        sent_ref[3 + d] = speeds[d]
        sent_ref[d] = leave_ref[d] + TIME_STEP * speeds[d]


def main_kernel(sec_ref, table_ref, cell_ref, base_ref, out_ref, hi_ref, lo_ref):
    sec = sec_ref[0]
    high, low = cell_split(cell_ref[...], sec)
    hi_ref[...] = high.astype(F32)
    lo_ref[...] = low.astype(F32)
    counts = counters()
    rows = cell_ref.shape[0]

    def step(i, carry):
        ats = [pl.ds(2 * i + h, 1) for h in range(2)]
        found = pick(table_ref, 4, [hi_ref[at, :] for at in ats], [lo_ref[at, :] for at in ats], counts)
        for f in range(4):
            for h in range(2):
                out_ref[f, ats[h], :] = found[f][h]
        return carry

    lax.fori_loop(0, rows // 2, step, 0)
    drag = TIME_STEP * out_ref[0] * base_ref[6]
    scale = 1.0 / (1.0 + drag)
    speeds = [(base_ref[3 + d] + drag * out_ref[1 + d]) * scale for d in range(3)]
    for d in range(3):
        out_ref[3 + d] = speeds[d]
        out_ref[d] = base_ref[d] + TIME_STEP * speeds[d]


def settle_kernel(
    dep_ref, mask_ref, moved_ref, a_ref, b_ref, c_ref, d_ref, pos_ref, vel_ref,
    hi_ref, lo_ref, left_ref, right_ref, keep_ref,
):
    dep = dep_ref[...]
    hi_ref[...] = (dep >> 7).astype(F32)
    lo_ref[...] = (dep & (LANES - 1)).astype(F32)
    counts = counters()
    movers = dep_ref.shape[1]
    per = movers // LANES
    arrivals = (b_ref, a_ref, d_ref, c_ref)
    for r in range(4):
        for q in range(per):
            left_ref[:, (r * per + q) * LANES : (r * per + q + 1) * LANES] = one_hot(
                hi_ref[r : r + 1, q * LANES : (q + 1) * LANES], counts
            )
    zero = jnp.zeros((16, LANES), BF16)
    for f in range(6):
        for r in range(4):
            for q in range(per):
                value = arrivals[r][f, q : q + 1, :]
                part = value.astype(BF16).astype(F32)
                va, vb = row16(part), row16(value - part)
                low = row16(lo_ref[r : r + 1, q * LANES : (q + 1) * LANES])
                hits = [low == c for c in counts]
                lanes = slice((r * per + q) * LANES, (r * per + q + 1) * LANES)
                right_ref[:, lanes] = jnp.concatenate(
                    [jnp.where(h, va, zero) for h in hits] + [jnp.where(h, vb, zero) for h in hits],
                    axis=0,
                )
        placed = lax.dot_general(left_ref[...], right_ref[...], NT, preferred_element_type=F32)
        placed = placed[:, :LANES] + placed[:, LANES:]
        keep_ref[f] = jnp.where(mask_ref[...] > 0.5, placed, moved_ref[f])

    def spread(b, carry):
        at = pl.ds(pl.multiple_of(b * LANES, LANES), LANES)
        for d in range(3):
            pos_ref[d : d + 1, at] = keep_ref[d, pl.ds(b, 1), :]
            vel_ref[d : d + 1, at] = keep_ref[3 + d, pl.ds(b, 1), :]
        return carry

    lax.fori_loop(0, moved_ref.shape[1], spread, 0, unroll=4)


def shifted(block, axis, distance):
    count = lax.axis_size(axis)
    return lax.ppermute(block, axis, [((i - distance) % count, i) for i in range(count)])


def body(pressure, fluid_velocity, positions, velocities, volumes, cells, partners, departures):
    particles = volumes.shape[0]
    rows = particles // LANES
    movers = departures.shape[1]
    sec = lax.axis_index("sec").astype(jnp.int32).reshape(1)
    vol2 = volumes.reshape(rows, LANES)
    cell2 = cells.reshape(rows, LANES)
    dense = pltpu.VMEM((rows, LANES), F32)

    (mine,) = call(
        deposit_kernel, [((384, LANES), F32)], sec, vol2, cell2, pressure, fluid_velocity,
        scratch=[dense] * 4, smem=(0,), flops=2 * particles * 128 * 256,
    )
    got = shifted(mine, "sec", 1)
    (base,) = call(
        contact_kernel, [((7, rows, LANES), F32)], vol2, positions, velocities, partners,
        flops=particles * 8 * 500,
    )
    tile, up, down = call(
        tile_kernel, [((10, 64, LANES), F32), ((10, 40, LANES), F32), ((10, 40, LANES), F32)], mine, got,
    )
    ylow = shifted(up, "gy", 1)
    yhigh = shifted(down, "gy", -1)
    leave, mask = call(
        leave_kernel, [((8, 4 * movers // LANES, LANES), F32), ((LANES, LANES), F32)],
        sec, base, cell2, departures,
        scratch=[
            pltpu.VMEM((4, movers), F32), pltpu.VMEM((4, movers), F32), pltpu.VMEM((8 * LANES, 2 * LANES), BF16),
        ],
        smem=(0,), flops=2 * 4 * movers * 1024 * 256,
    )
    xup, xdown = call(
        side_kernel, [((10, 80, LANES), F32), ((10, 80, LANES), F32)], tile, ylow, yhigh,
    )
    xlow = shifted(xup, "gx", 1)
    xhigh = shifted(xdown, "gx", -1)
    size = 8 + 2 * HALO
    grid = pltpu.VMEM((size, 24, 2 * LANES), F32)
    p_out, v_out, table, sent = call(
        fluid_kernel,
        [
            (pressure.shape, F32), (fluid_velocity.shape, F32), ((4 * LANES, 2 * LANES), BF16),
            ((6, 4 * movers // LANES, LANES), F32),
        ],
        tile, ylow, yhigh, xlow, xhigh, leave,
        scratch=[pltpu.VMEM((5, size, 24, 2 * LANES), F32), grid, grid, grid, pltpu.VMEM((4, size, 24, 2 * LANES), F32)],
        flops=2 * 4 * movers * 512 * 256,
    )
    per = movers // LANES
    arrived = [
        shifted(sent[:, row * per : (row + 1) * per], axis, offset)
        for row, axis, offset in ((0, "gx", 1), (1, "gx", -1), (2, "gy", 1), (3, "gy", -1))
    ]
    (moved,) = call(
        main_kernel, [((6, rows, LANES), F32)], sec, table, cell2, base,
        scratch=[dense] * 2, smem=(0,), flops=2 * particles * 512 * 256,
    )
    pos_out, vel_out = call(
        settle_kernel, [(positions.shape, F32), (velocities.shape, F32)],
        departures, mask, moved, *arrived,
        scratch=[
            pltpu.VMEM((4, movers), F32), pltpu.VMEM((4, movers), F32),
            pltpu.VMEM((LANES, 4 * movers), BF16), pltpu.VMEM((2 * LANES, 4 * movers), BF16),
            pltpu.VMEM((6, rows, LANES), F32),
        ],
        flops=2 * 4 * movers * 128 * 1536,
    )
    return p_out, v_out, pos_out, vel_out


def solution(mesh):
    placed = (
        P("gx", "gy", "sec"),
        P(None, "gx", "gy", "sec"),
        P(None, ("gx", "gy", "sec")),
        P(None, ("gx", "gy", "sec")),
        P(("gx", "gy", "sec")),
        P(("gx", "gy", "sec")),
        P(None, ("gx", "gy", "sec")),
        P(None, ("gx", "gy", "sec")),
    )
    return jax.shard_map(
        body,
        mesh=mesh,
        in_specs=placed,
        out_specs=(
            P("gx", "gy", "sec"),
            P(None, "gx", "gy", "sec"),
            P(None, ("gx", "gy", "sec")),
            P(None, ("gx", "gy", "sec")),
        ),
        check_vma=False,
    )
```

```python
import jax
import jax.numpy as jnp
from jax import lax
from jax.experimental import pallas as pl
from jax.experimental.pallas import tpu as pltpu
from jax.sharding import PartitionSpec as P

SWEEPS = 4
PAIRS = 8
BLOCK = 128
LANES = 128
HALO = SWEEPS + 1

TIME_STEP = 0.1
RELAX_RATE = 0.5
DAMPING = 0.5
RANGE_SQUARED = 16.0
GRAVITY = 1.0

F32 = jnp.float32
BF16 = jnp.bfloat16
NT = (((1,), (1,)), ((), ()))


def call(kernel, outs, *args, scratch=(), busy_us=0.1, smem=(), loose=()):
    outs_list = [jax.ShapeDtypeStruct(shape, dtype) for shape, dtype in outs]
    vmem = pl.BlockSpec(memory_space=pltpu.VMEM)
    scalar = pl.BlockSpec(memory_space=pltpu.SMEM)
    anywhere = pl.BlockSpec(memory_space=pl.ANY)
    specs = [scalar if i in smem else anywhere if i in loose else vmem for i in range(len(args))]
    return pl.pallas_call(
        kernel,
        out_shape=outs_list,
        in_specs=specs,
        out_specs=[vmem] * len(outs_list),
        scratch_shapes=list(scratch),
        compiler_params=pltpu.CompilerParams(vmem_limit_bytes=24 * 1024 * 1024),
        cost_estimate=pl.CostEstimate(flops=int(busy_us * 1.15e9), bytes_accessed=4096, transcendentals=0),
    )(*args)


def split(values):
    high = values.astype(BF16)
    return high, (values - high.astype(F32)).astype(BF16)


def row16(row):
    return jnp.broadcast_to(row, (16, row.shape[1])).astype(BF16)


def counters():
    base = lax.broadcasted_iota(jnp.int32, (16, LANES), 0)
    return [(base + 16 * k).astype(F32).astype(BF16) for k in range(8)]


def one_hot(row, counts, values=None):
    wide = row16(row)
    zero = jnp.zeros((16, LANES), BF16)
    if values is None:
        values = jnp.ones((16, LANES), BF16)
    return jnp.concatenate([jnp.where(wide == c, values, zero) for c in counts], axis=0)


def cell_split(cells, sec):
    high = (cells >> 8) + 64 * (((cells >> 7) & 1) ^ sec)
    return high, cells & (LANES - 1)


def deposit_kernel(
    sec_ref, vol_in, cell_in, out_ref, vol_ref, cell_ref, hi_ref, lo_ref, va_ref, vb_ref, sems,
):
    copies = [
        pltpu.make_async_copy(vol_in, vol_ref, sems.at[0]),
        pltpu.make_async_copy(cell_in, cell_ref, sems.at[1]),
    ]
    for copy in copies:
        copy.start()
    for copy in copies:
        copy.wait()
    sec = sec_ref[0]
    high, low = cell_split(cell_ref[...], sec)
    hi_ref[...] = high.astype(F32)
    lo_ref[...] = low.astype(F32)
    vol = vol_ref[...]
    part = vol.astype(BF16).astype(F32)
    va_ref[...] = part
    vb_ref[...] = vol - part
    counts = counters()
    zero = jnp.zeros((16, LANES), BF16)
    rows_each = 16
    steps = vol_ref.shape[0] // rows_each

    def step(i, acc):
        lefts, rights = [], []
        for r in range(rows_each):
            at = pl.ds(i * rows_each + r, 1)
            lefts.append(one_hot(hi_ref[at, :], counts))
            low_row = row16(lo_ref[at, :])
            va, vb = row16(va_ref[at, :]), row16(vb_ref[at, :])
            hits = [low_row == c for c in counts]
            rights.append(
                jnp.concatenate(
                    [jnp.where(h, va, zero) for h in hits] + [jnp.where(h, vb, zero) for h in hits],
                    axis=0,
                )
            )
        left = jnp.concatenate(lefts, axis=1)
        right = jnp.concatenate(rights, axis=1)
        return acc + lax.dot_general(left, right, NT, preferred_element_type=F32)

    acc = lax.fori_loop(0, steps, step, jnp.zeros((LANES, 2 * LANES), F32), unroll=2)
    out_ref[...] = acc[:, :LANES] + acc[:, LANES:]


def contact_kernel(vol_ref, pos_ref, vel_ref, pair_ref, after_ref, base_ref):
    blocks = pos_ref.shape[1] // BLOCK
    base_ref[6] = RELAX_RATE * jnp.exp((-2.0 / 3.0) * jnp.log(vol_ref[...]))

    def step(b, carry):
        at = pl.ds(pl.multiple_of(b * BLOCK, BLOCK), BLOCK)
        index = pair_ref[:, at]
        mine = [pos_ref[d : d + 1, at] for d in range(3)] + [vel_ref[d : d + 1, at] for d in range(3)]
        wide = [jnp.broadcast_to(m, (PAIRS, BLOCK)) for m in mine]
        other = [jnp.take_along_axis(w, index, axis=1, mode="promise_in_bounds") for w in wide]
        apart = [wide[d] - other[d] for d in range(3)]
        dist = apart[0] * apart[0] + apart[1] * apart[1] + apart[2] * apart[2]
        weight = 1.0 / (1.0 + dist * (1.0 / RANGE_SQUARED))
        for d in range(3):
            push = weight * (apart[d] + DAMPING * (other[3 + d] - wide[3 + d]))
            force = jnp.sum(push, axis=0, keepdims=True)
            if d == 0:
                force = force - GRAVITY
            base_ref[d, pl.ds(b, 1), :] = mine[d]
            base_ref[3 + d, pl.ds(b, 1), :] = mine[3 + d] + TIME_STEP * force
        return carry

    lax.fori_loop(0, blocks, step, 0, unroll=8)


def table_of(fields, table_ref):
    for f, values in enumerate(fields):
        high, low = split(jnp.swapaxes(values, 0, 1))
        table_ref[f * LANES : (f + 1) * LANES, :LANES] = high
        table_ref[f * LANES : (f + 1) * LANES, LANES:] = low


def pick(table_ref, fields, high_rows, low_rows, counts):
    hot = jnp.concatenate([one_hot(row, counts) for row in high_rows], axis=1)
    hot = jnp.concatenate([hot, hot], axis=0)
    lane = lax.broadcasted_iota(jnp.int32, (LANES, LANES), 0).astype(F32)
    hits = [jnp.broadcast_to(row, (LANES, LANES)) == lane for row in low_rows]
    found = []
    for f in range(fields):
        rows = jnp.dot(table_ref[f * LANES : (f + 1) * LANES, :], hot, preferred_element_type=F32)
        found.append(
            [
                jnp.sum(jnp.where(hit, rows[:, LANES * h : LANES * (h + 1)], 0.0), axis=0, keepdims=True)
                for h, hit in enumerate(hits)
            ]
        )
    return found


def leave_kernel(
    sec_ref, base_ref, cell_ref, dep_ref, after_ref, out_ref, mask_ref, left_ref, low_ref, hi_ref, lo_ref, table_ref
):
    sec = sec_ref[0]
    high, low = cell_split(cell_ref[...], sec)
    cell = (high * LANES + low).astype(F32)
    table_of([base_ref[f] for f in range(7)] + [cell], table_ref)
    counts = counters()
    per = dep_ref.shape[1] // LANES
    for r in range(4):
        for q in range(per):
            row = dep_ref[r : r + 1, q * LANES : (q + 1) * LANES]
            k = r * per + q
            hi_row, lo_row = (row >> 7).astype(F32), (row & (LANES - 1)).astype(F32)
            hi_ref[k : k + 1, :] = hi_row
            lo_ref[k : k + 1, :] = lo_row
            left_ref[:, k * LANES : (k + 1) * LANES] = one_hot(hi_row, counts)
            low_ref[:, k * LANES : (k + 1) * LANES] = one_hot(lo_row, counts)

    def step(i, carry):
        ats = [pl.ds(2 * i + h, 1) for h in range(2)]
        found = pick(table_ref, 8, [hi_ref[at, :] for at in ats], [lo_ref[at, :] for at in ats], counts)
        for f in range(8):
            for h in range(2):
                out_ref[f, ats[h], :] = found[f][h]
        return carry

    lax.fori_loop(0, 2 * per, step, 0, unroll=8)
    mask_ref[...] = lax.dot_general(left_ref[...], low_ref[...], NT, preferred_element_type=F32)


def slices_y(tile_ref, fields, up_ref, down_ref):
    for g in range(fields):
        for j in range(HALO):
            up_ref[g, 8 * j : 8 * j + 8, :] = tile_ref[g, pl.ds(8 - HALO + j, 8, stride=8), :]
            down_ref[g, 8 * j : 8 * j + 8, :] = tile_ref[g, pl.ds(j, 8, stride=8), :]


def early_kernel(p_ref, v_ref, far_p_ref, far_v_ref, tile_ref, up_ref, down_ref):
    tile_ref[0] = p_ref[...]
    tile_ref[1] = far_p_ref[...]
    for d in range(3):
        tile_ref[2 + 2 * d] = v_ref[64 * d : 64 * d + 64, :]
        tile_ref[3 + 2 * d] = far_v_ref[64 * d : 64 * d + 64, :]
    slices_y(tile_ref, 8, up_ref, down_ref)


def tile_kernel(mine_ref, got_ref, after_ref, tile_ref, up_ref, down_ref):
    own = mine_ref[0:64, :] + got_ref[64:128, :]
    far = mine_ref[64:128, :] + got_ref[0:64, :]
    tile_ref[0] = 1.0 / (1.0 + own)
    tile_ref[1] = 1.0 / (1.0 + far)
    slices_y(tile_ref, 2, up_ref, down_ref)


def side_kernel(tile_ref, low_ref, high_ref, after_ref, up_ref, down_ref):
    for g in range(tile_ref.shape[0]):
        for x in range(8):
            slab = jnp.concatenate(
                [
                    low_ref[g, pl.ds(8 + x, 4, stride=8), :],
                    tile_ref[g, 8 * x : 8 * x + 8, :],
                    high_ref[g, pl.ds(x, 4, stride=8), :],
                ],
                axis=0,
            )
            if x >= 8 - HALO:
                at = x - (8 - HALO)
                up_ref[g, 16 * at : 16 * at + 16, :] = slab
            if x < HALO:
                down_ref[g, 16 * x : 16 * x + 16, :] = slab


def assemble(tile_ref, ylow_ref, yhigh_ref, xlow_ref, xhigh_ref, grid_ref):
    filler = jnp.ones((8, LANES), F32)
    for g in range(tile_ref.shape[0]):
        f, h = g // 2, g % 2
        lanes = slice(LANES * h, LANES * (h + 1))
        for j in range(HALO):
            grid_ref[f, j, 0:16, lanes] = xlow_ref[g, 16 * j : 16 * j + 16, :]
            grid_ref[f, j, 16:24, lanes] = filler
            grid_ref[f, 8 + HALO + j, 0:16, lanes] = xhigh_ref[g, 16 * j : 16 * j + 16, :]
            grid_ref[f, 8 + HALO + j, 16:24, lanes] = filler
        for x in range(8):
            grid_ref[f, HALO + x, 0:24, lanes] = jnp.concatenate(
                [
                    ylow_ref[g, pl.ds(8 + x, 4, stride=8), :],
                    tile_ref[g, 8 * x : 8 * x + 8, :],
                    yhigh_ref[g, pl.ds(x, 5, stride=8), :],
                    filler[:6],
                    ylow_ref[g, x : x + 1, :],
                ],
                axis=0,
            )


def y_sides(values):
    return pltpu.roll(values, 23, 0), pltpu.roll(values, 1, 0)


def z_sides(values):
    return pltpu.roll(values, 2 * LANES - 1, 1), pltpu.roll(values, 1, 1)


def fluid_kernel(
    tile_ref, ylow_ref, yhigh_ref, xlow_ref, xhigh_ref, flow_ref, leave_ref,
    p_out_ref, v_out_ref, table_ref, sent_ref,
    void_ref, even_ref, odd_ref, invd_ref, div_ref, face_ref,
):
    size = 8 + 2 * HALO
    assemble(tile_ref, ylow_ref, yhigh_ref, xlow_ref, xhigh_ref, void_ref)

    for x in range(1, size - 1):
        void = void_ref[0, x]
        above, below = void_ref[0, x + 1], void_ref[0, x - 1]
        sides = y_sides(void) + z_sides(void)
        total = 6.0 * void + above + below
        for k in range(4):
            total = total + sides[k]
            face_ref[k, x] = void + sides[k]
        invd_ref[x] = 1.0 / total
        ys = y_sides(void * flow_ref[2, x])
        zs = z_sides(void * flow_ref[3, x])
        div_ref[x] = (
            above * flow_ref[1, x + 1] - below * flow_ref[1, x - 1] + (ys[0] - ys[1]) + (zs[0] - zs[1])
        )

    for t in range(SWEEPS):
        source = flow_ref.at[0] if t == 0 else even_ref if t % 2 == 0 else odd_ref
        target = odd_ref if t % 2 == 0 else even_ref
        for x in range(1 + t, size - 1 - t):
            void = void_ref[0, x]
            values = source[x]
            sides = y_sides(values) + z_sides(values)
            total = (void + void_ref[0, x + 1]) * source[x + 1] - div_ref[x]
            total = total + (void + void_ref[0, x - 1]) * source[x - 1]
            for k in range(4):
                total = total + face_ref[k, x] * sides[k]
            target[x] = total * invd_ref[x]

    final = even_ref if SWEEPS % 2 == 0 else odd_ref
    tables = [[], [], [], []]
    for x in range(8):
        values = final[HALO + x]
        ys, zs = y_sides(values), z_sides(values)
        flows = (
            flow_ref[1, HALO + x] - 0.5 * (final[HALO + x + 1] - final[HALO + x - 1]),
            flow_ref[2, HALO + x] - 0.5 * (ys[0] - ys[1]),
            flow_ref[3, HALO + x] - 0.5 * (zs[0] - zs[1]),
        )
        p_out_ref[x] = values[4:12, :LANES]
        tables[0].append(jnp.exp(-2.65 * jnp.log(void_ref[0, HALO + x][4:12])))
        for d in range(3):
            kept = flows[d][4:12]
            v_out_ref[d, x] = kept[:, :LANES]
            tables[1 + d].append(kept)
    fields = []
    for f in range(4):
        whole = jnp.concatenate(tables[f], axis=0)
        fields.append(jnp.concatenate([whole[:, :LANES], whole[:, LANES:]], axis=0))
    table_of(fields, table_ref)

    counts = counters()
    count = leave_ref.shape[1]

    def step(i, carry):
        his, los = [], []
        for h in range(2):
            cell = leave_ref[7, pl.ds(2 * i + h, 1), :].astype(jnp.int32)
            his.append((cell >> 7).astype(F32))
            los.append((cell & (LANES - 1)).astype(F32))
        found = pick(table_ref, 4, his, los, counts)
        for f in range(4):
            for h in range(2):
                sent_ref[f, pl.ds(2 * i + h, 1), :] = found[f][h]
        return carry

    lax.fori_loop(0, count // 2, step, 0, unroll=8)
    drag = TIME_STEP * sent_ref[0] * leave_ref[6]
    scale = 1.0 / (1.0 + drag)
    speeds = [(leave_ref[3 + d] + drag * sent_ref[1 + d]) * scale for d in range(3)]
    for d in range(3):
        sent_ref[3 + d] = speeds[d]
        sent_ref[d] = leave_ref[d] + TIME_STEP * speeds[d]


def flow_kernel(tile_ref, ylow_ref, yhigh_ref, xlow_ref, xhigh_ref, flow_ref):
    assemble(tile_ref, ylow_ref, yhigh_ref, xlow_ref, xhigh_ref, flow_ref)


def main_kernel(sec_ref, table_ref, cell_ref, base_ref, out_ref, hi_ref, lo_ref):
    sec = sec_ref[0]
    high, low = cell_split(cell_ref[...], sec)
    hi_ref[...] = high.astype(F32)
    lo_ref[...] = low.astype(F32)
    counts = counters()
    rows = cell_ref.shape[0]

    def step(i, carry):
        ats = [pl.ds(2 * i + h, 1) for h in range(2)]
        found = pick(table_ref, 4, [hi_ref[at, :] for at in ats], [lo_ref[at, :] for at in ats], counts)
        for f in range(4):
            for h in range(2):
                out_ref[f, ats[h], :] = found[f][h]
        return carry

    lax.fori_loop(0, rows // 2, step, 0, unroll=16)
    drag = TIME_STEP * out_ref[0] * base_ref[6]
    scale = 1.0 / (1.0 + drag)
    speeds = [(base_ref[3 + d] + drag * out_ref[1 + d]) * scale for d in range(3)]
    for d in range(3):
        out_ref[3 + d] = speeds[d]
        out_ref[d] = base_ref[d] + TIME_STEP * speeds[d]


def settle_kernel(
    left_ref, low_ref, mask_ref, moved_ref, a_ref, b_ref, c_ref, d_ref, pos_ref, vel_ref, right_ref, keep_ref,
):
    per = a_ref.shape[1]
    arrivals = (b_ref, a_ref, d_ref, c_ref)
    stays = mask_ref[...] < 0.5
    for f in range(6):
        for r in range(4):
            for q in range(per):
                value = arrivals[r][f, q : q + 1, :]
                part = value.astype(BF16).astype(F32)
                lanes = slice((r * per + q) * LANES, (r * per + q + 1) * LANES)
                for k, wide in enumerate((row16(part), row16(value - part))):
                    for m in range(8):
                        right_ref[f % 2, LANES * k + 16 * m : LANES * k + 16 * m + 16, lanes] = (
                            low_ref[16 * m : 16 * m + 16, lanes] * wide
                        )
        placed = lax.dot_general(left_ref[...], right_ref[f % 2], NT, preferred_element_type=F32)
        placed = placed[:, :LANES] + placed[:, LANES:]
        keep_ref[f] = jnp.where(stays, moved_ref[f], placed)

    def spread(b, carry):
        at = pl.ds(pl.multiple_of(b * LANES, LANES), LANES)
        for d in range(3):
            pos_ref[d : d + 1, at] = keep_ref[d, pl.ds(b, 1), :]
            vel_ref[d : d + 1, at] = keep_ref[3 + d, pl.ds(b, 1), :]
        return carry

    lax.fori_loop(0, moved_ref.shape[1], spread, 0, unroll=16)


def shifted(block, axis, distance):
    count = lax.axis_size(axis)
    return lax.ppermute(block, axis, [((i - distance) % count, i) for i in range(count)])


def body(pressure, fluid_velocity, positions, velocities, volumes, cells, partners, departures):
    particles = volumes.shape[0]
    rows = particles // LANES
    movers = departures.shape[1]
    sec = lax.axis_index("sec").astype(jnp.int32).reshape(1)
    vol2 = volumes.reshape(rows, LANES)
    cell2 = cells.reshape(rows, LANES)
    near_p = pressure.reshape(64, LANES)
    near_v = fluid_velocity.reshape(192, LANES)
    dense = pltpu.VMEM((rows, LANES), F32)
    size = 8 + 2 * HALO
    leavers = 4 * movers // LANES

    far_p = shifted(near_p, "sec", 1)
    far_v = shifted(near_v, "sec", 1)
    (mine,) = call(
        deposit_kernel, [((LANES, LANES), F32)], sec, vol2, cell2,
        scratch=[dense, pltpu.VMEM((rows, LANES), jnp.int32)] + [dense] * 4 + [pltpu.SemaphoreType.DMA((2,))],
        smem=(0,), loose=(1, 2), busy_us=4,
    )
    got = shifted(mine, "sec", 1)
    state, state_up, state_down = call(
        early_kernel, [((8, 64, LANES), F32), ((8, 40, LANES), F32), ((8, 40, LANES), F32)],
        near_p, near_v, far_p, far_v,
    )
    state_ylow = shifted(state_up, "gy", 1)
    state_yhigh = shifted(state_down, "gy", -1)
    (base,) = call(
        contact_kernel, [((7, rows, LANES), F32)], vol2, positions, velocities, partners, state,
        loose=(4,), busy_us=4,
    )
    tile, up, down = call(
        tile_kernel, [((2, 64, LANES), F32), ((2, 40, LANES), F32), ((2, 40, LANES), F32)], mine, got, base,
        loose=(2,),
    )
    ylow = shifted(up, "gy", 1)
    yhigh = shifted(down, "gy", -1)
    state_xup, state_xdown = call(
        side_kernel, [((8, 80, LANES), F32), ((8, 80, LANES), F32)], state, state_ylow, state_yhigh, up, loose=(3,),
    )
    state_xlow = shifted(state_xup, "gx", 1)
    state_xhigh = shifted(state_xdown, "gx", -1)
    leave, mask, left, low = call(
        leave_kernel,
        [
            ((8, leavers, LANES), F32), ((LANES, LANES), F32), ((LANES, 4 * movers), BF16),
            ((LANES, 4 * movers), BF16),
        ],
        sec, base, cell2, departures, state_xup,
        scratch=[
            pltpu.VMEM((leavers, LANES), F32), pltpu.VMEM((leavers, LANES), F32),
            pltpu.VMEM((8 * LANES, 2 * LANES), BF16),
        ],
        smem=(0,), loose=(4,), busy_us=4,
    )
    xup, xdown = call(
        side_kernel, [((2, 80, LANES), F32), ((2, 80, LANES), F32)], tile, ylow, yhigh, leave, loose=(3,),
    )
    xlow = shifted(xup, "gx", 1)
    xhigh = shifted(xdown, "gx", -1)
    (flow,) = call(
        flow_kernel, [((4, size, 24, 2 * LANES), F32)], state, state_ylow, state_yhigh, state_xlow, state_xhigh,
        busy_us=1,
    )
    grid = pltpu.VMEM((size, 24, 2 * LANES), F32)
    p_out, v_out, table, sent = call(
        fluid_kernel,
        [
            (pressure.shape, F32), (fluid_velocity.shape, F32), ((4 * LANES, 2 * LANES), BF16),
            ((6, leavers, LANES), F32),
        ],
        tile, ylow, yhigh, xlow, xhigh, flow, leave,
        scratch=[
            pltpu.VMEM((1, size, 24, 2 * LANES), F32), grid, grid, grid, grid,
            pltpu.VMEM((4, size, 24, 2 * LANES), F32),
        ],
        busy_us=6,
    )
    per = movers // LANES
    arrived = [
        shifted(sent[:, row * per : (row + 1) * per], axis, offset)
        for row, axis, offset in ((0, "gx", 1), (1, "gx", -1), (2, "gy", 1), (3, "gy", -1))
    ]
    (moved,) = call(
        main_kernel, [((6, rows, LANES), F32)], sec, table, cell2, base,
        scratch=[dense] * 2, smem=(0,), busy_us=6,
    )
    pos_out, vel_out = call(
        settle_kernel, [(positions.shape, F32), (velocities.shape, F32)],
        left, low, mask, moved, *arrived,
        scratch=[pltpu.VMEM((2, 2 * LANES, 4 * movers), BF16), pltpu.VMEM((6, rows, LANES), F32)],
        busy_us=4,
    )
    return p_out, v_out, pos_out, vel_out


def solution(mesh):
    placed = (
        P("gx", "gy", "sec"),
        P(None, "gx", "gy", "sec"),
        P(None, ("gx", "gy", "sec")),
        P(None, ("gx", "gy", "sec")),
        P(("gx", "gy", "sec")),
        P(("gx", "gy", "sec")),
        P(None, ("gx", "gy", "sec")),
        P(None, ("gx", "gy", "sec")),
    )
    return jax.shard_map(
        body,
        mesh=mesh,
        in_specs=placed,
        out_specs=(
            P("gx", "gy", "sec"),
            P(None, "gx", "gy", "sec"),
            P(None, ("gx", "gy", "sec")),
            P(None, ("gx", "gy", "sec")),
        ),
        check_vma=False,
    )
```

```python
import functools

import jax
import jax.numpy as jnp
from jax import lax
from jax.experimental import pallas as pl
from jax.experimental.pallas import tpu as pltpu
from jax.sharding import PartitionSpec as P

SWEEPS = 4
PAIRS = 8
BLOCK = 128
LANES = 128
HALO = SWEEPS + 1

TIME_STEP = 0.1
RELAX_RATE = 0.5
DAMPING = 0.5
RANGE_SQUARED = 16.0
GRAVITY = 1.0

F32 = jnp.float32
BF16 = jnp.bfloat16
NT = (((1,), (1,)), ((), ()))


def call(kernel, outs, *args, scratch=(), busy_us=0.1, smem=(), loose=(), hbm=()):
    outs_list = [jax.ShapeDtypeStruct(shape, dtype) for shape, dtype in outs]
    vmem = pl.BlockSpec(memory_space=pltpu.VMEM)
    scalar = pl.BlockSpec(memory_space=pltpu.SMEM)
    anywhere = pl.BlockSpec(memory_space=pl.ANY)
    outside = pl.BlockSpec(memory_space=pltpu.HBM)
    specs = [
        scalar if i in smem else anywhere if i in loose else outside if i in hbm else vmem
        for i in range(len(args))
    ]
    return pl.pallas_call(
        kernel,
        out_shape=outs_list,
        in_specs=specs,
        out_specs=[vmem] * len(outs_list),
        scratch_shapes=list(scratch),
        compiler_params=pltpu.CompilerParams(vmem_limit_bytes=24 * 1024 * 1024),
        cost_estimate=pl.CostEstimate(flops=int(busy_us * 1.15e9), bytes_accessed=4096, transcendentals=0),
    )(*args)


def split(values):
    high = values.astype(BF16)
    return high, (values - high.astype(F32)).astype(BF16)


def row16(row):
    return jnp.broadcast_to(row, (16, row.shape[1])).astype(BF16)


def counters():
    base = lax.broadcasted_iota(jnp.int32, (16, LANES), 0)
    return [(base + 16 * k).astype(F32).astype(BF16) for k in range(8)]


def one_hot(row, counts, values=None):
    wide = row16(row)
    zero = jnp.zeros((16, LANES), BF16)
    if values is None:
        values = jnp.ones((16, LANES), BF16)
    return jnp.concatenate([jnp.where(wide == c, values, zero) for c in counts], axis=0)


def cell_split(cells, sec):
    high = (cells >> 8) + 64 * (((cells >> 7) & 1) ^ sec)
    return high, cells & (LANES - 1)


def deposit_kernel(
    sec_ref, vol_in, cell_in, out_ref, vol_ref, cell_ref, hi_ref, lo_ref, va_ref, vb_ref, sems,
):
    copies = [
        pltpu.make_async_copy(vol_in, vol_ref, sems.at[0]),
        pltpu.make_async_copy(cell_in, cell_ref, sems.at[1]),
    ]
    for copy in copies:
        copy.start()
    for copy in copies:
        copy.wait()
    sec = sec_ref[0]
    high, low = cell_split(cell_ref[...], sec)
    hi_ref[...] = high.astype(F32)
    lo_ref[...] = low.astype(F32)
    vol = vol_ref[...]
    part = vol.astype(BF16).astype(F32)
    va_ref[...] = part
    vb_ref[...] = vol - part
    counts = counters()
    zero = jnp.zeros((16, LANES), BF16)
    rows_each = 16
    steps = vol_ref.shape[0] // rows_each

    def step(i, acc):
        lefts, rights = [], []
        for r in range(rows_each):
            at = pl.ds(i * rows_each + r, 1)
            lefts.append(one_hot(hi_ref[at, :], counts))
            low_row = row16(lo_ref[at, :])
            va, vb = row16(va_ref[at, :]), row16(vb_ref[at, :])
            hits = [low_row == c for c in counts]
            rights.append(
                jnp.concatenate(
                    [jnp.where(h, va, zero) for h in hits] + [jnp.where(h, vb, zero) for h in hits],
                    axis=0,
                )
            )
        left = jnp.concatenate(lefts, axis=1)
        right = jnp.concatenate(rights, axis=1)
        return acc + lax.dot_general(left, right, NT, preferred_element_type=F32)

    acc = lax.fori_loop(0, steps, step, jnp.zeros((LANES, 2 * LANES), F32), unroll=2)
    out_ref[...] = acc[:, :LANES] + acc[:, LANES:]


def contact_kernel(vol_ref, pos_ref, vel_ref, pair_ref, after_ref, base_ref):
    blocks = pos_ref.shape[1] // BLOCK
    base_ref[6] = RELAX_RATE * jnp.exp((-2.0 / 3.0) * jnp.log(vol_ref[...]))

    def step(b, carry):
        at = pl.ds(pl.multiple_of(b * BLOCK, BLOCK), BLOCK)
        index = pair_ref[:, at]
        mine = [pos_ref[d : d + 1, at] for d in range(3)] + [vel_ref[d : d + 1, at] for d in range(3)]
        wide = [jnp.broadcast_to(m, (PAIRS, BLOCK)) for m in mine]
        other = [jnp.take_along_axis(w, index, axis=1, mode="promise_in_bounds") for w in wide]
        apart = [wide[d] - other[d] for d in range(3)]
        dist = apart[0] * apart[0] + apart[1] * apart[1] + apart[2] * apart[2]
        weight = 1.0 / (1.0 + dist * (1.0 / RANGE_SQUARED))
        for d in range(3):
            push = weight * (apart[d] + DAMPING * (other[3 + d] - wide[3 + d]))
            force = jnp.sum(push, axis=0, keepdims=True)
            if d == 0:
                force = force - GRAVITY
            base_ref[d, pl.ds(b, 1), :] = mine[d]
            base_ref[3 + d, pl.ds(b, 1), :] = mine[3 + d] + TIME_STEP * force
        return carry

    lax.fori_loop(0, blocks, step, 0, unroll=8)


def table_of(fields, table_ref):
    for f, values in enumerate(fields):
        high, low = split(jnp.swapaxes(values, 0, 1))
        table_ref[f * LANES : (f + 1) * LANES, :LANES] = high
        table_ref[f * LANES : (f + 1) * LANES, LANES:] = low


def pick(table_ref, fields, high_rows, low_rows, counts):
    hot = jnp.concatenate([one_hot(row, counts) for row in high_rows], axis=1)
    hot = jnp.concatenate([hot, hot], axis=0)
    lane = lax.broadcasted_iota(jnp.int32, (LANES, LANES), 0).astype(F32)
    hits = [jnp.broadcast_to(row, (LANES, LANES)) == lane for row in low_rows]
    found = []
    for f in range(fields):
        rows = jnp.dot(table_ref[f * LANES : (f + 1) * LANES, :], hot, preferred_element_type=F32)
        found.append(
            [
                jnp.sum(jnp.where(hit, rows[:, LANES * h : LANES * (h + 1)], 0.0), axis=0, keepdims=True)
                for h, hit in enumerate(hits)
            ]
        )
    return found


def marks_kernel(dep_ref, after_ref, mask_ref, left_ref, low_ref):
    counts = counters()
    per = dep_ref.shape[1] // LANES
    for r in range(4):
        for q in range(per):
            row = dep_ref[r : r + 1, q * LANES : (q + 1) * LANES]
            hi_row, lane = (row >> 7).astype(F32), row & (LANES - 1)
            lanes = slice((r * per + q) * LANES, (r * per + q + 1) * LANES)
            for h in range(2):
                left_ref[h * LANES : (h + 1) * LANES, lanes] = one_hot(
                    jnp.where((lane >> 6) == h, hi_row, -1.0), counts
                )
            low_ref[:, lanes] = one_hot((lane & 63).astype(F32), counts[:4])
    mask_ref[...] = unfold(lax.dot_general(low_ref[...], left_ref[...], NT, preferred_element_type=F32))


def unfold(halves):
    return jnp.swapaxes(jnp.concatenate([halves[:, :LANES], halves[:, LANES:]], axis=0), 0, 1)


def leave_kernel(sec_ref, base_ref, cell_ref, dep_ref, after_ref, out_ref, hi_ref, lo_ref, table_ref):
    sec = sec_ref[0]
    high, low = cell_split(cell_ref[...], sec)
    cell = (high * LANES + low).astype(F32)
    table_of([base_ref[f] for f in range(7)] + [cell], table_ref)
    counts = counters()
    per = dep_ref.shape[1] // LANES
    for r in range(4):
        for q in range(per):
            row = dep_ref[r : r + 1, q * LANES : (q + 1) * LANES]
            k = r * per + q
            hi_ref[k : k + 1, :] = (row >> 7).astype(F32)
            lo_ref[k : k + 1, :] = (row & (LANES - 1)).astype(F32)

    def step(i, carry):
        ats = [pl.ds(2 * i + h, 1) for h in range(2)]
        found = pick(table_ref, 8, [hi_ref[at, :] for at in ats], [lo_ref[at, :] for at in ats], counts)
        for f in range(8):
            for h in range(2):
                out_ref[f, ats[h], :] = found[f][h]
        return carry

    lax.fori_loop(0, 2 * per, step, 0, unroll=8)


STATE = ((HALO, HALO, HALO), (HALO - 1, HALO, HALO), (HALO, HALO - 1, HALO), (HALO - 1, HALO - 1, HALO - 1))
VOID = ((HALO, HALO, HALO),)


def y_starts(spec):
    starts, at = [], 0
    for depth, _, _ in spec:
        for _ in range(2):
            starts.append(at)
            at += 8 * depth
    return starts, at


def x_starts(spec):
    starts, at = [], 0
    for _, depth, reach in spec:
        for _ in range(2):
            own = []
            for away in range(1, depth + 1):
                extra = min(HALO - 1, reach - away)
                own.append((at, extra))
                at += 8 + 2 * extra
            starts.append(own)
    return starts, at


def slices_y(spec, tile_ref, up_ref, down_ref):
    for g, start in enumerate(y_starts(spec)[0]):
        depth = spec[g // 2][0]
        for j in range(depth):
            at = start + 8 * j
            up_ref[at : at + 8, :] = tile_ref[g, pl.ds(8 - depth + j, 8, stride=8), :]
            down_ref[at : at + 8, :] = tile_ref[g, pl.ds(j, 8, stride=8), :]


def early_kernel(p_ref, v_ref, far_p_ref, far_v_ref, tile_ref, up_ref, down_ref):
    tile_ref[0] = p_ref[...]
    tile_ref[1] = far_p_ref[...]
    for d in range(3):
        tile_ref[2 + 2 * d] = v_ref[64 * d : 64 * d + 64, :]
        tile_ref[3 + 2 * d] = far_v_ref[64 * d : 64 * d + 64, :]
    slices_y(STATE, tile_ref, up_ref, down_ref)


def tile_kernel(mine_ref, got_ref, after_ref, tile_ref, up_ref, down_ref):
    own = mine_ref[0:64, :] + got_ref[64:128, :]
    far = mine_ref[64:128, :] + got_ref[0:64, :]
    tile_ref[0] = 1.0 / (1.0 + own)
    tile_ref[1] = 1.0 / (1.0 + far)
    slices_y(VOID, tile_ref, up_ref, down_ref)


def side_kernel(spec, tile_ref, low_ref, high_ref, after_ref, up_ref, down_ref):
    starts = x_starts(spec)[0]
    for g, y_start in enumerate(y_starts(spec)[0]):
        depth = spec[g // 2][0]
        for away, (start, extra) in enumerate(starts[g], 1):
            for x, out_ref in ((8 - away, up_ref), (away - 1, down_ref)):
                rows = [tile_ref[g, 8 * x : 8 * x + 8, :]]
                if extra > 0:
                    rows.insert(0, low_ref[pl.ds(y_start + 8 * (depth - extra) + x, extra, stride=8), :])
                    rows.append(high_ref[pl.ds(y_start + x, extra, stride=8), :])
                rows = jnp.concatenate(rows, axis=0) if extra > 0 else rows[0]
                out_ref[start : start + 8 + 2 * extra, :] = rows


def assemble(spec, tile_ref, ylow_ref, yhigh_ref, xlow_ref, xhigh_ref, grid_ref):
    filler = jnp.ones((8, LANES), F32)
    starts = x_starts(spec)[0]
    for g, y_start in enumerate(y_starts(spec)[0]):
        f, h = g // 2, g % 2
        depth = spec[f][0]
        lanes = slice(LANES * h, LANES * (h + 1))
        for x in list(range(HALO)) + list(range(HALO + 8, 2 * HALO + 8)):
            for m in range(3):
                grid_ref[f, x, 8 * m : 8 * m + 8, lanes] = filler
        for away, (start, extra) in enumerate(starts[g], 1):
            for x, side_ref in ((HALO - away, xlow_ref), (HALO + 7 + away, xhigh_ref)):
                grid_ref[f, x, 4 - extra : 12 + extra, lanes] = side_ref[start : start + 8 + 2 * extra, :]
        for x in range(8):
            far = depth - 4
            rows = [
                ylow_ref[pl.ds(y_start + 8 * far + x, 4, stride=8), :],
                tile_ref[g, 8 * x : 8 * x + 8, :],
                yhigh_ref[pl.ds(y_start + x, depth, stride=8), :],
                filler[: 8 - 2 * far],
            ]
            if far > 0:
                rows.append(ylow_ref[y_start + x : y_start + x + 1, :])
            grid_ref[f, HALO + x, 0:24, lanes] = jnp.concatenate(rows, axis=0)


def y_sides(values):
    return pltpu.roll(values, 23, 0), pltpu.roll(values, 1, 0)


def z_sides(values):
    return pltpu.roll(values, 2 * LANES - 1, 1), pltpu.roll(values, 1, 1)


def fluid_kernel(
    tile_ref, ylow_ref, yhigh_ref, xlow_ref, xhigh_ref, flow_ref, leave_ref,
    p_out_ref, v_out_ref, table_ref, sent_ref,
    void_ref, even_ref, odd_ref, invd_ref, div_ref, face_ref,
):
    size = 8 + 2 * HALO
    assemble(VOID, tile_ref, ylow_ref, yhigh_ref, xlow_ref, xhigh_ref, void_ref)

    for x in range(1, size - 1):
        void = void_ref[0, x]
        above, below = void_ref[0, x + 1], void_ref[0, x - 1]
        sides = y_sides(void) + z_sides(void)
        total = 6.0 * void + above + below
        for k in range(4):
            total = total + sides[k]
            face_ref[k, x] = void + sides[k]
        invd_ref[x] = 1.0 / total
        ys = y_sides(void * flow_ref[2, x])
        zs = z_sides(void * flow_ref[3, x])
        div_ref[x] = (
            above * flow_ref[1, x + 1] - below * flow_ref[1, x - 1] + (ys[0] - ys[1]) + (zs[0] - zs[1])
        )

    for t in range(SWEEPS):
        source = flow_ref.at[0] if t == 0 else even_ref if t % 2 == 0 else odd_ref
        target = odd_ref if t % 2 == 0 else even_ref
        for x in range(1 + t, size - 1 - t):
            void = void_ref[0, x]
            values = source[x]
            sides = y_sides(values) + z_sides(values)
            total = (void + void_ref[0, x + 1]) * source[x + 1] - div_ref[x]
            total = total + (void + void_ref[0, x - 1]) * source[x - 1]
            for k in range(4):
                total = total + face_ref[k, x] * sides[k]
            target[x] = total * invd_ref[x]

    final = even_ref if SWEEPS % 2 == 0 else odd_ref
    tables = [[], [], [], []]
    for x in range(8):
        values = final[HALO + x]
        ys, zs = y_sides(values), z_sides(values)
        flows = (
            flow_ref[1, HALO + x] - 0.5 * (final[HALO + x + 1] - final[HALO + x - 1]),
            flow_ref[2, HALO + x] - 0.5 * (ys[0] - ys[1]),
            flow_ref[3, HALO + x] - 0.5 * (zs[0] - zs[1]),
        )
        p_out_ref[x] = values[4:12, :LANES]
        tables[0].append(jnp.exp(-2.65 * jnp.log(void_ref[0, HALO + x][4:12])))
        for d in range(3):
            kept = flows[d][4:12]
            v_out_ref[d, x] = kept[:, :LANES]
            tables[1 + d].append(kept)
    fields = []
    for f in range(4):
        whole = jnp.concatenate(tables[f], axis=0)
        fields.append(jnp.concatenate([whole[:, :LANES], whole[:, LANES:]], axis=0))
    table_of(fields, table_ref)

    counts = counters()
    count = leave_ref.shape[1]

    def step(i, carry):
        his, los = [], []
        for h in range(2):
            cell = leave_ref[7, pl.ds(2 * i + h, 1), :].astype(jnp.int32)
            his.append((cell >> 7).astype(F32))
            los.append((cell & (LANES - 1)).astype(F32))
        found = pick(table_ref, 4, his, los, counts)
        for f in range(4):
            for h in range(2):
                sent_ref[f, pl.ds(2 * i + h, 1), :] = found[f][h]
        return carry

    lax.fori_loop(0, count // 2, step, 0, unroll=8)
    drag = TIME_STEP * sent_ref[0] * leave_ref[6]
    scale = 1.0 / (1.0 + drag)
    speeds = [(leave_ref[3 + d] + drag * sent_ref[1 + d]) * scale for d in range(3)]
    for d in range(3):
        sent_ref[3 + d] = speeds[d]
        sent_ref[d] = leave_ref[d] + TIME_STEP * speeds[d]


def flow_kernel(tile_ref, ylow_ref, yhigh_ref, xlow_ref, xhigh_ref, flow_ref):
    assemble(STATE, tile_ref, ylow_ref, yhigh_ref, xlow_ref, xhigh_ref, flow_ref)


def main_kernel(sec_ref, table_ref, cell_ref, base_ref, out_ref, hi_ref, lo_ref):
    sec = sec_ref[0]
    high, low = cell_split(cell_ref[...], sec)
    hi_ref[...] = high.astype(F32)
    lo_ref[...] = low.astype(F32)
    counts = counters()
    rows = cell_ref.shape[0]

    def step(i, carry):
        ats = [pl.ds(2 * i + h, 1) for h in range(2)]
        found = pick(table_ref, 4, [hi_ref[at, :] for at in ats], [lo_ref[at, :] for at in ats], counts)
        for f in range(4):
            for h in range(2):
                out_ref[f, ats[h], :] = found[f][h]
        return carry

    lax.fori_loop(0, rows // 2, step, 0, unroll=16)
    drag = TIME_STEP * out_ref[0] * base_ref[6]
    scale = 1.0 / (1.0 + drag)
    speeds = [(base_ref[3 + d] + drag * out_ref[1 + d]) * scale for d in range(3)]
    for d in range(3):
        out_ref[3 + d] = speeds[d]
        out_ref[d] = base_ref[d] + TIME_STEP * speeds[d]


def settle_kernel(
    left_ref, low_ref, mask_ref, moved_ref, a_ref, b_ref, c_ref, d_ref, pos_ref, vel_ref, right_ref, keep_ref,
):
    per = a_ref.shape[1]
    arrivals = (b_ref, a_ref, d_ref, c_ref)
    stays = mask_ref[...] < 0.5
    for f in range(6):
        for r in range(4):
            for q in range(per):
                value = arrivals[r][f, q : q + 1, :]
                part = value.astype(BF16).astype(F32)
                lanes = slice((r * per + q) * LANES, (r * per + q + 1) * LANES)
                for k, wide in enumerate((row16(part), row16(value - part))):
                    for m in range(4):
                        at = LANES * f + 64 * k + 16 * m
                        right_ref[at : at + 16, lanes] = low_ref[16 * m : 16 * m + 16, lanes] * wide
    placed = lax.dot_general(right_ref[...], left_ref[...], NT, preferred_element_type=F32)
    for f in range(6):
        rows = unfold(placed[LANES * f : LANES * f + 64] + placed[LANES * f + 64 : LANES * f + 128])
        keep_ref[f] = jnp.where(stays, moved_ref[f], rows)

    def spread(b, carry):
        at = pl.ds(pl.multiple_of(b * LANES, LANES), LANES)
        for d in range(3):
            pos_ref[d : d + 1, at] = keep_ref[d, pl.ds(b, 1), :]
            vel_ref[d : d + 1, at] = keep_ref[3 + d, pl.ds(b, 1), :]
        return carry

    lax.fori_loop(0, moved_ref.shape[1], spread, 0, unroll=16)


def shifted(block, axis, distance):
    count = lax.axis_size(axis)
    return lax.ppermute(block, axis, [((i - distance) % count, i) for i in range(count)])


def body(pressure, fluid_velocity, positions, velocities, volumes, cells, partners, departures):
    particles = volumes.shape[0]
    rows = particles // LANES
    movers = departures.shape[1]
    sec = lax.axis_index("sec").astype(jnp.int32).reshape(1)
    vol2 = volumes.reshape(rows, LANES)
    cell2 = cells.reshape(rows, LANES)
    near_p = pressure.reshape(64, LANES)
    near_v = fluid_velocity.reshape(192, LANES)
    dense = pltpu.VMEM((rows, LANES), F32)
    size = 8 + 2 * HALO
    leavers = 4 * movers // LANES

    far_p = shifted(near_p, "sec", 1)
    far_v = shifted(near_v, "sec", 1)
    (mine,) = call(
        deposit_kernel, [((LANES, LANES), F32)], sec, vol2, cell2,
        scratch=[dense, pltpu.VMEM((rows, LANES), jnp.int32)] + [dense] * 4 + [pltpu.SemaphoreType.DMA((2,))],
        smem=(0,), hbm=(1, 2), busy_us=4,
    )
    got = shifted(mine, "sec", 1)
    state_y, state_x = y_starts(STATE)[1], x_starts(STATE)[1]
    void_y, void_x = y_starts(VOID)[1], x_starts(VOID)[1]
    state, state_up, state_down = call(
        early_kernel, [((8, 64, LANES), F32), ((state_y, LANES), F32), ((state_y, LANES), F32)],
        near_p, near_v, far_p, far_v,
    )
    state_ylow = shifted(state_up, "gy", 1)
    state_yhigh = shifted(state_down, "gy", -1)
    (base,) = call(
        contact_kernel, [((7, rows, LANES), F32)], vol2, positions, velocities, partners, state,
        loose=(4,), busy_us=4,
    )
    tile, up, down = call(
        tile_kernel, [((2, 64, LANES), F32), ((void_y, LANES), F32), ((void_y, LANES), F32)], mine, got, base,
        loose=(2,),
    )
    ylow = shifted(up, "gy", 1)
    yhigh = shifted(down, "gy", -1)
    state_xup, state_xdown = call(
        functools.partial(side_kernel, STATE), [((state_x, LANES), F32), ((state_x, LANES), F32)],
        state, state_ylow, state_yhigh, up, loose=(3,),
    )
    state_xlow = shifted(state_xup, "gx", 1)
    state_xhigh = shifted(state_xdown, "gx", -1)
    mask, left, low = call(
        marks_kernel, [((rows, LANES), F32), ((2 * LANES, 4 * movers), BF16), ((64, 4 * movers), BF16)],
        departures, state_xup, loose=(1,), busy_us=2,
    )
    xup, xdown = call(
        functools.partial(side_kernel, VOID), [((void_x, LANES), F32), ((void_x, LANES), F32)],
        tile, ylow, yhigh, mask, loose=(3,),
    )
    xlow = shifted(xup, "gx", 1)
    xhigh = shifted(xdown, "gx", -1)
    (leave,) = call(
        leave_kernel, [((8, leavers, LANES), F32)], sec, base, cell2, departures, xup,
        scratch=[
            pltpu.VMEM((leavers, LANES), F32), pltpu.VMEM((leavers, LANES), F32),
            pltpu.VMEM((8 * LANES, 2 * LANES), BF16),
        ],
        smem=(0,), loose=(4,), busy_us=3,
    )
    (flow,) = call(
        flow_kernel, [((4, size, 24, 2 * LANES), F32)], state, state_ylow, state_yhigh, state_xlow, state_xhigh, busy_us=1,
    )
    grid = pltpu.VMEM((size, 24, 2 * LANES), F32)
    p_out, v_out, table, sent = call(
        fluid_kernel,
        [
            (pressure.shape, F32), (fluid_velocity.shape, F32), ((4 * LANES, 2 * LANES), BF16),
            ((6, leavers, LANES), F32),
        ],
        tile, ylow, yhigh, xlow, xhigh, flow, leave,
        scratch=[
            pltpu.VMEM((1, size, 24, 2 * LANES), F32), grid, grid, grid, grid,
            pltpu.VMEM((4, size, 24, 2 * LANES), F32),
        ],
        busy_us=6,
    )
    per = movers // LANES
    arrived = [
        shifted(sent[:, row * per : (row + 1) * per], axis, offset)
        for row, axis, offset in ((0, "gx", 1), (1, "gx", -1), (2, "gy", 1), (3, "gy", -1))
    ]
    (moved,) = call(
        main_kernel, [((6, rows, LANES), F32)], sec, table, cell2, base,
        scratch=[dense] * 2, smem=(0,), busy_us=6,
    )
    pos_out, vel_out = call(
        settle_kernel, [(positions.shape, F32), (velocities.shape, F32)],
        left, low, mask, moved, *arrived,
        scratch=[pltpu.VMEM((6 * LANES, 4 * movers), BF16), pltpu.VMEM((6, rows, LANES), F32)],
        busy_us=4,
    )
    return p_out, v_out, pos_out, vel_out


def solution(mesh):
    placed = (
        P("gx", "gy", "sec"),
        P(None, "gx", "gy", "sec"),
        P(None, ("gx", "gy", "sec")),
        P(None, ("gx", "gy", "sec")),
        P(("gx", "gy", "sec")),
        P(("gx", "gy", "sec")),
        P(None, ("gx", "gy", "sec")),
        P(None, ("gx", "gy", "sec")),
    )
    return jax.shard_map(
        body,
        mesh=mesh,
        in_specs=placed,
        out_specs=(
            P("gx", "gy", "sec"),
            P(None, "gx", "gy", "sec"),
            P(None, ("gx", "gy", "sec")),
            P(None, ("gx", "gy", "sec")),
        ),
        check_vma=False,
    )
```

```python
import functools

import jax
import jax.numpy as jnp
from jax import lax
from jax.experimental import pallas as pl
from jax.experimental.pallas import tpu as pltpu
from jax.sharding import PartitionSpec as P

SWEEPS = 4
PAIRS = 8
BLOCK = 128
LANES = 128
HALO = SWEEPS + 1

TIME_STEP = 0.1
RELAX_RATE = 0.5
DAMPING = 0.5
RANGE_SQUARED = 16.0
GRAVITY = 1.0

F32 = jnp.float32
BF16 = jnp.bfloat16
NT = (((1,), (1,)), ((), ()))


def call(kernel, outs, *args, scratch=(), busy_us=0.1, smem=(), loose=()):
    outs_list = [jax.ShapeDtypeStruct(shape, dtype) for shape, dtype in outs]
    vmem = pl.BlockSpec(memory_space=pltpu.VMEM)
    scalar = pl.BlockSpec(memory_space=pltpu.SMEM)
    anywhere = pl.BlockSpec(memory_space=pl.ANY)
    specs = [scalar if i in smem else anywhere if i in loose else vmem for i in range(len(args))]
    return pl.pallas_call(
        kernel,
        out_shape=outs_list,
        in_specs=specs,
        out_specs=[vmem] * len(outs_list),
        scratch_shapes=list(scratch),
        compiler_params=pltpu.CompilerParams(vmem_limit_bytes=24 * 1024 * 1024),
        cost_estimate=pl.CostEstimate(flops=int(busy_us * 1.15e9), bytes_accessed=4096, transcendentals=0),
    )(*args)


def split(values):
    high = values.astype(BF16)
    return high, (values - high.astype(F32)).astype(BF16)


def row16(row):
    return jnp.broadcast_to(row, (16, row.shape[1])).astype(BF16)


def counters():
    base = lax.broadcasted_iota(jnp.int32, (16, LANES), 0)
    return [(base + 16 * k).astype(F32).astype(BF16) for k in range(8)]


def one_hot(row, counts, values=None):
    wide = row16(row)
    zero = jnp.zeros((16, LANES), BF16)
    if values is None:
        values = jnp.ones((16, LANES), BF16)
    return jnp.concatenate([jnp.where(wide == c, values, zero) for c in counts], axis=0)


def cell_split(cells, sec):
    high = (cells >> 8) + 64 * (((cells >> 7) & 1) ^ sec)
    return high, cells & (LANES - 1)


def ahead_kernel(out_ref):
    out_ref[...] = jnp.zeros(out_ref.shape, F32)


def deposit_kernel(sec_ref, vol_ref, cell_ref, after_ref, out_ref, hi_ref, lo_ref, va_ref, vb_ref):
    sec = sec_ref[0]
    high, low = cell_split(cell_ref[...], sec)
    hi_ref[...] = high.astype(F32)
    lo_ref[...] = low.astype(F32)
    vol = vol_ref[...]
    part = vol.astype(BF16).astype(F32)
    va_ref[...] = part
    vb_ref[...] = vol - part
    counts = counters()
    zero = jnp.zeros((16, LANES), BF16)
    rows_each = 16
    steps = vol_ref.shape[0] // rows_each

    def step(i, acc):
        lefts, rights = [], []
        for r in range(rows_each):
            at = pl.ds(i * rows_each + r, 1)
            lefts.append(one_hot(hi_ref[at, :], counts))
            low_row = row16(lo_ref[at, :])
            va, vb = row16(va_ref[at, :]), row16(vb_ref[at, :])
            hits = [low_row == c for c in counts]
            rights.append(
                jnp.concatenate(
                    [jnp.where(h, va, zero) for h in hits] + [jnp.where(h, vb, zero) for h in hits],
                    axis=0,
                )
            )
        left = jnp.concatenate(lefts, axis=1)
        right = jnp.concatenate(rights, axis=1)
        return acc + lax.dot_general(left, right, NT, preferred_element_type=F32)

    acc = lax.fori_loop(0, steps, step, jnp.zeros((LANES, 2 * LANES), F32), unroll=4)
    out_ref[...] = acc[:, :LANES] + acc[:, LANES:]


def contact_kernel(vol_ref, pos_ref, vel_ref, pair_ref, after_ref, base_ref):
    blocks = pos_ref.shape[1] // BLOCK
    base_ref[6] = RELAX_RATE * jnp.exp((-2.0 / 3.0) * jnp.log(vol_ref[...]))

    def step(b, carry):
        at = pl.ds(pl.multiple_of(b * BLOCK, BLOCK), BLOCK)
        index = pair_ref[:, at]
        mine = [pos_ref[d : d + 1, at] for d in range(3)] + [vel_ref[d : d + 1, at] for d in range(3)]
        wide = [jnp.broadcast_to(m, (PAIRS, BLOCK)) for m in mine]
        other = [jnp.take_along_axis(w, index, axis=1, mode="promise_in_bounds") for w in wide]
        apart = [wide[d] - other[d] for d in range(3)]
        dist = apart[0] * apart[0] + apart[1] * apart[1] + apart[2] * apart[2]
        weight = 1.0 / (1.0 + dist * (1.0 / RANGE_SQUARED))
        for d in range(3):
            push = weight * (apart[d] + DAMPING * (other[3 + d] - wide[3 + d]))
            force = jnp.sum(push, axis=0, keepdims=True)
            if d == 0:
                force = force - GRAVITY
            base_ref[d, pl.ds(b, 1), :] = mine[d]
            base_ref[3 + d, pl.ds(b, 1), :] = mine[3 + d] + TIME_STEP * force
        return carry

    lax.fori_loop(0, blocks, step, 0, unroll=32)


def table_of(fields, table_ref):
    for f, values in enumerate(fields):
        high, low = split(jnp.swapaxes(values, 0, 1))
        table_ref[f * LANES : (f + 1) * LANES, :LANES] = high
        table_ref[f * LANES : (f + 1) * LANES, LANES:] = low


def pick(table_ref, fields, high_rows, low_rows, counts):
    hot = jnp.concatenate([one_hot(row, counts) for row in high_rows], axis=1)
    hot = jnp.concatenate([hot, hot], axis=0)
    lane = lax.broadcasted_iota(jnp.int32, (LANES, LANES), 0).astype(F32)
    hits = [jnp.broadcast_to(row, (LANES, LANES)) == lane for row in low_rows]
    found = []
    for f in range(fields):
        rows = jnp.dot(table_ref[f * LANES : (f + 1) * LANES, :], hot, preferred_element_type=F32)
        found.append(
            [
                jnp.sum(jnp.where(hit, rows[:, LANES * h : LANES * (h + 1)], 0.0), axis=0, keepdims=True)
                for h, hit in enumerate(hits)
            ]
        )
    return found


def marks_kernel(dep_ref, after_ref, mask_ref, left_ref, low_ref):
    counts = counters()
    per = dep_ref.shape[1] // LANES
    for r in range(4):
        for q in range(per):
            row = dep_ref[r : r + 1, q * LANES : (q + 1) * LANES]
            hi_row, lane = (row >> 7).astype(F32), row & (LANES - 1)
            lanes = slice((r * per + q) * LANES, (r * per + q + 1) * LANES)
            for h in range(2):
                left_ref[h * LANES : (h + 1) * LANES, lanes] = one_hot(
                    jnp.where((lane >> 6) == h, hi_row, -1.0), counts
                )
            low_ref[:, lanes] = one_hot((lane & 63).astype(F32), counts[:4])
    mask_ref[...] = unfold(lax.dot_general(low_ref[...], left_ref[...], NT, preferred_element_type=F32))


def unfold(halves):
    return jnp.swapaxes(jnp.concatenate([halves[:, :LANES], halves[:, LANES:]], axis=0), 0, 1)


def leave_kernel(sec_ref, base_ref, cell_ref, dep_ref, after_ref, out_ref, hi_ref, lo_ref, table_ref):
    sec = sec_ref[0]
    high, low = cell_split(cell_ref[...], sec)
    cell = (high * LANES + low).astype(F32)
    table_of([base_ref[f] for f in range(7)] + [cell], table_ref)
    counts = counters()
    per = dep_ref.shape[1] // LANES
    for r in range(4):
        for q in range(per):
            row = dep_ref[r : r + 1, q * LANES : (q + 1) * LANES]
            k = r * per + q
            hi_ref[k : k + 1, :] = (row >> 7).astype(F32)
            lo_ref[k : k + 1, :] = (row & (LANES - 1)).astype(F32)

    def step(i, carry):
        ats = [pl.ds(2 * i + h, 1) for h in range(2)]
        found = pick(table_ref, 8, [hi_ref[at, :] for at in ats], [lo_ref[at, :] for at in ats], counts)
        for f in range(8):
            for h in range(2):
                out_ref[f, ats[h], :] = found[f][h]
        return carry

    lax.fori_loop(0, 2 * per, step, 0, unroll=16)


STATE = ((HALO, HALO, HALO), (HALO - 1, HALO, HALO), (HALO, HALO - 1, HALO), (HALO - 1, HALO - 1, HALO - 1))
VOID = ((HALO, HALO, HALO),)


def y_starts(spec):
    starts, at = [], 0
    for depth, _, _ in spec:
        for _ in range(2):
            starts.append(at)
            at += 8 * depth
    return starts, at


def x_starts(spec):
    starts, at = [], 0
    for _, depth, reach in spec:
        for _ in range(2):
            own = []
            for away in range(1, depth + 1):
                extra = min(HALO - 1, reach - away)
                own.append((at, extra))
                at += 8 + 2 * extra
            starts.append(own)
    return starts, at


def slices_y(spec, tile_ref, up_ref, down_ref):
    for g, start in enumerate(y_starts(spec)[0]):
        depth = spec[g // 2][0]
        for j in range(depth):
            at = start + 8 * j
            up_ref[at : at + 8, :] = tile_ref[g, pl.ds(8 - depth + j, 8, stride=8), :]
            down_ref[at : at + 8, :] = tile_ref[g, pl.ds(j, 8, stride=8), :]


def early_kernel(p_ref, v_ref, far_p_ref, far_v_ref, tile_ref, up_ref, down_ref):
    tile_ref[0] = p_ref[...]
    tile_ref[1] = far_p_ref[...]
    for d in range(3):
        tile_ref[2 + 2 * d] = v_ref[64 * d : 64 * d + 64, :]
        tile_ref[3 + 2 * d] = far_v_ref[64 * d : 64 * d + 64, :]
    slices_y(STATE, tile_ref, up_ref, down_ref)


def tile_kernel(mine_ref, got_ref, after_ref, tile_ref, up_ref, down_ref):
    own = mine_ref[0:64, :] + got_ref[64:128, :]
    far = mine_ref[64:128, :] + got_ref[0:64, :]
    tile_ref[0] = 1.0 / (1.0 + own)
    tile_ref[1] = 1.0 / (1.0 + far)
    slices_y(VOID, tile_ref, up_ref, down_ref)


def side_kernel(spec, tile_ref, low_ref, high_ref, after_ref, up_ref, down_ref):
    starts = x_starts(spec)[0]
    for g, y_start in enumerate(y_starts(spec)[0]):
        depth = spec[g // 2][0]
        for away, (start, extra) in enumerate(starts[g], 1):
            for x, out_ref in ((8 - away, up_ref), (away - 1, down_ref)):
                rows = [tile_ref[g, 8 * x : 8 * x + 8, :]]
                if extra > 0:
                    rows.insert(0, low_ref[pl.ds(y_start + 8 * (depth - extra) + x, extra, stride=8), :])
                    rows.append(high_ref[pl.ds(y_start + x, extra, stride=8), :])
                rows = jnp.concatenate(rows, axis=0) if extra > 0 else rows[0]
                out_ref[start : start + 8 + 2 * extra, :] = rows


def assemble(spec, tile_ref, ylow_ref, yhigh_ref, xlow_ref, xhigh_ref, grid_ref):
    filler = jnp.ones((8, LANES), F32)
    starts = x_starts(spec)[0]
    for g, y_start in enumerate(y_starts(spec)[0]):
        f, h = g // 2, g % 2
        depth = spec[f][0]
        lanes = slice(LANES * h, LANES * (h + 1))
        for x in list(range(HALO)) + list(range(HALO + 8, 2 * HALO + 8)):
            for m in range(3):
                grid_ref[f, x, 8 * m : 8 * m + 8, lanes] = filler
        for away, (start, extra) in enumerate(starts[g], 1):
            for x, side_ref in ((HALO - away, xlow_ref), (HALO + 7 + away, xhigh_ref)):
                grid_ref[f, x, 4 - extra : 12 + extra, lanes] = side_ref[start : start + 8 + 2 * extra, :]
        for x in range(8):
            far = depth - 4
            rows = [
                ylow_ref[pl.ds(y_start + 8 * far + x, 4, stride=8), :],
                tile_ref[g, 8 * x : 8 * x + 8, :],
                yhigh_ref[pl.ds(y_start + x, depth, stride=8), :],
                filler[: 8 - 2 * far],
            ]
            if far > 0:
                rows.append(ylow_ref[y_start + x : y_start + x + 1, :])
            grid_ref[f, HALO + x, 0:24, lanes] = jnp.concatenate(rows, axis=0)


def y_sides(values):
    return pltpu.roll(values, 23, 0), pltpu.roll(values, 1, 0)


def z_sides(values):
    return pltpu.roll(values, 2 * LANES - 1, 1), pltpu.roll(values, 1, 1)


def fluid_kernel(
    tile_ref, ylow_ref, yhigh_ref, xlow_ref, xhigh_ref, flow_ref, leave_ref,
    p_out_ref, v_out_ref, table_ref, sent_ref,
    void_ref, even_ref, odd_ref, invd_ref, div_ref, face_ref,
):
    size = 8 + 2 * HALO
    assemble(VOID, tile_ref, ylow_ref, yhigh_ref, xlow_ref, xhigh_ref, void_ref)

    for x in range(1, size - 1):
        void = void_ref[0, x]
        above, below = void_ref[0, x + 1], void_ref[0, x - 1]
        sides = y_sides(void) + z_sides(void)
        total = 6.0 * void + above + below
        for k in range(4):
            total = total + sides[k]
            face_ref[k, x] = void + sides[k]
        invd_ref[x] = 1.0 / total
        ys = y_sides(void * flow_ref[2, x])
        zs = z_sides(void * flow_ref[3, x])
        div_ref[x] = (
            above * flow_ref[1, x + 1] - below * flow_ref[1, x - 1] + (ys[0] - ys[1]) + (zs[0] - zs[1])
        )

    for t in range(SWEEPS):
        source = flow_ref.at[0] if t == 0 else even_ref if t % 2 == 0 else odd_ref
        target = odd_ref if t % 2 == 0 else even_ref
        for x in range(1 + t, size - 1 - t):
            void = void_ref[0, x]
            values = source[x]
            sides = y_sides(values) + z_sides(values)
            total = (void + void_ref[0, x + 1]) * source[x + 1] - div_ref[x]
            total = total + (void + void_ref[0, x - 1]) * source[x - 1]
            for k in range(4):
                total = total + face_ref[k, x] * sides[k]
            target[x] = total * invd_ref[x]

    final = even_ref if SWEEPS % 2 == 0 else odd_ref
    tables = [[], [], [], []]
    for x in range(8):
        values = final[HALO + x]
        ys, zs = y_sides(values), z_sides(values)
        flows = (
            flow_ref[1, HALO + x] - 0.5 * (final[HALO + x + 1] - final[HALO + x - 1]),
            flow_ref[2, HALO + x] - 0.5 * (ys[0] - ys[1]),
            flow_ref[3, HALO + x] - 0.5 * (zs[0] - zs[1]),
        )
        p_out_ref[x] = values[4:12, :LANES]
        tables[0].append(jnp.exp(-2.65 * jnp.log(void_ref[0, HALO + x][4:12])))
        for d in range(3):
            kept = flows[d][4:12]
            v_out_ref[d, x] = kept[:, :LANES]
            tables[1 + d].append(kept)
    fields = []
    for f in range(4):
        whole = jnp.concatenate(tables[f], axis=0)
        fields.append(jnp.concatenate([whole[:, :LANES], whole[:, LANES:]], axis=0))
    table_of(fields, table_ref)

    counts = counters()
    count = leave_ref.shape[1]

    def step(i, carry):
        his, los = [], []
        for h in range(2):
            cell = leave_ref[7, pl.ds(2 * i + h, 1), :].astype(jnp.int32)
            his.append((cell >> 7).astype(F32))
            los.append((cell & (LANES - 1)).astype(F32))
        found = pick(table_ref, 4, his, los, counts)
        for f in range(4):
            for h in range(2):
                sent_ref[f, pl.ds(2 * i + h, 1), :] = found[f][h]
        return carry

    lax.fori_loop(0, count // 2, step, 0, unroll=16)
    drag = TIME_STEP * sent_ref[0] * leave_ref[6]
    scale = 1.0 / (1.0 + drag)
    speeds = [(leave_ref[3 + d] + drag * sent_ref[1 + d]) * scale for d in range(3)]
    for d in range(3):
        sent_ref[3 + d] = speeds[d]
        sent_ref[d] = leave_ref[d] + TIME_STEP * speeds[d]


def flow_kernel(tile_ref, ylow_ref, yhigh_ref, xlow_ref, xhigh_ref, flow_ref):
    assemble(STATE, tile_ref, ylow_ref, yhigh_ref, xlow_ref, xhigh_ref, flow_ref)


def main_kernel(sec_ref, table_ref, cell_ref, base_ref, out_ref, hi_ref, lo_ref):
    sec = sec_ref[0]
    high, low = cell_split(cell_ref[...], sec)
    hi_ref[...] = high.astype(F32)
    lo_ref[...] = low.astype(F32)
    counts = counters()
    rows = cell_ref.shape[0]

    def step(i, carry):
        ats = [pl.ds(2 * i + h, 1) for h in range(2)]
        found = pick(table_ref, 4, [hi_ref[at, :] for at in ats], [lo_ref[at, :] for at in ats], counts)
        for f in range(4):
            for h in range(2):
                out_ref[f, ats[h], :] = found[f][h]
        return carry

    lax.fori_loop(0, rows // 2, step, 0, unroll=32)
    drag = TIME_STEP * out_ref[0] * base_ref[6]
    scale = 1.0 / (1.0 + drag)
    speeds = [(base_ref[3 + d] + drag * out_ref[1 + d]) * scale for d in range(3)]
    for d in range(3):
        out_ref[3 + d] = speeds[d]
        out_ref[d] = base_ref[d] + TIME_STEP * speeds[d]


def settle_kernel(
    left_ref, low_ref, mask_ref, moved_ref, a_ref, b_ref, c_ref, d_ref, pos_ref, vel_ref, right_ref, keep_ref,
):
    per = a_ref.shape[1]
    arrivals = (b_ref, a_ref, d_ref, c_ref)
    stays = mask_ref[...] < 0.5
    for f in range(6):
        for r in range(4):
            for q in range(per):
                value = arrivals[r][f, q : q + 1, :]
                part = value.astype(BF16).astype(F32)
                lanes = slice((r * per + q) * LANES, (r * per + q + 1) * LANES)
                for k, wide in enumerate((row16(part), row16(value - part))):
                    for m in range(4):
                        at = LANES * f + 64 * k + 16 * m
                        right_ref[at : at + 16, lanes] = low_ref[16 * m : 16 * m + 16, lanes] * wide
    placed = lax.dot_general(right_ref[...], left_ref[...], NT, preferred_element_type=F32)
    for f in range(6):
        rows = unfold(placed[LANES * f : LANES * f + 64] + placed[LANES * f + 64 : LANES * f + 128])
        keep_ref[f] = jnp.where(stays, moved_ref[f], rows)

    def spread(b, carry):
        at = pl.ds(pl.multiple_of(b * LANES, LANES), LANES)
        for d in range(3):
            pos_ref[d : d + 1, at] = keep_ref[d, pl.ds(b, 1), :]
            vel_ref[d : d + 1, at] = keep_ref[3 + d, pl.ds(b, 1), :]
        return carry

    lax.fori_loop(0, moved_ref.shape[1], spread, 0, unroll=16)


def shifted(block, axis, distance):
    count = lax.axis_size(axis)
    return lax.ppermute(block, axis, [((i - distance) % count, i) for i in range(count)])


def body(pressure, fluid_velocity, positions, velocities, volumes, cells, partners, departures):
    particles = volumes.shape[0]
    rows = particles // LANES
    movers = departures.shape[1]
    sec = lax.axis_index("sec").astype(jnp.int32).reshape(1)
    vol2 = volumes.reshape(rows, LANES)
    cell2 = cells.reshape(rows, LANES)
    near_p = pressure.reshape(64, LANES)
    near_v = fluid_velocity.reshape(192, LANES)
    dense = pltpu.VMEM((rows, LANES), F32)
    size = 8 + 2 * HALO
    leavers = 4 * movers // LANES

    far_p = shifted(near_p, "sec", 1)
    far_v = shifted(near_v, "sec", 1)
    (ahead,) = call(ahead_kernel, [((8, LANES), F32)], busy_us=3)
    (mine,) = call(
        deposit_kernel, [((LANES, LANES), F32)], sec, vol2, cell2, ahead,
        scratch=[dense] * 4, smem=(0,), loose=(3,), busy_us=4,
    )
    got = shifted(mine, "sec", 1)
    state_y, state_x = y_starts(STATE)[1], x_starts(STATE)[1]
    void_y, void_x = y_starts(VOID)[1], x_starts(VOID)[1]
    state, state_up, state_down = call(
        early_kernel, [((8, 64, LANES), F32), ((state_y, LANES), F32), ((state_y, LANES), F32)],
        near_p, near_v, far_p, far_v,
    )
    state_ylow = shifted(state_up, "gy", 1)
    state_yhigh = shifted(state_down, "gy", -1)
    (base,) = call(
        contact_kernel, [((7, rows, LANES), F32)], vol2, positions, velocities, partners, state,
        loose=(4,), busy_us=4,
    )
    tile, up, down = call(
        tile_kernel, [((2, 64, LANES), F32), ((void_y, LANES), F32), ((void_y, LANES), F32)], mine, got, base,
        loose=(2,),
    )
    ylow = shifted(up, "gy", 1)
    yhigh = shifted(down, "gy", -1)
    state_xup, state_xdown = call(
        functools.partial(side_kernel, STATE), [((state_x, LANES), F32), ((state_x, LANES), F32)],
        state, state_ylow, state_yhigh, up, loose=(3,),
    )
    state_xlow = shifted(state_xup, "gx", 1)
    state_xhigh = shifted(state_xdown, "gx", -1)
    mask, left, low = call(
        marks_kernel, [((rows, LANES), F32), ((2 * LANES, 4 * movers), BF16), ((64, 4 * movers), BF16)],
        departures, state_xup, loose=(1,), busy_us=2,
    )
    xup, xdown = call(
        functools.partial(side_kernel, VOID), [((void_x, LANES), F32), ((void_x, LANES), F32)],
        tile, ylow, yhigh, mask, loose=(3,),
    )
    xlow = shifted(xup, "gx", 1)
    xhigh = shifted(xdown, "gx", -1)
    (leave,) = call(
        leave_kernel, [((8, leavers, LANES), F32)], sec, base, cell2, departures, xup,
        scratch=[
            pltpu.VMEM((leavers, LANES), F32), pltpu.VMEM((leavers, LANES), F32),
            pltpu.VMEM((8 * LANES, 2 * LANES), BF16),
        ],
        smem=(0,), loose=(4,), busy_us=3,
    )
    (flow,) = call(
        flow_kernel, [((4, size, 24, 2 * LANES), F32)], state, state_ylow, state_yhigh, state_xlow, state_xhigh, busy_us=1,
    )
    grid = pltpu.VMEM((size, 24, 2 * LANES), F32)
    p_out, v_out, table, sent = call(
        fluid_kernel,
        [
            (pressure.shape, F32), (fluid_velocity.shape, F32), ((4 * LANES, 2 * LANES), BF16),
            ((6, leavers, LANES), F32),
        ],
        tile, ylow, yhigh, xlow, xhigh, flow, leave,
        scratch=[
            pltpu.VMEM((1, size, 24, 2 * LANES), F32), grid, grid, grid, grid,
            pltpu.VMEM((4, size, 24, 2 * LANES), F32),
        ],
        busy_us=6,
    )
    per = movers // LANES
    arrived = [
        shifted(sent[:, row * per : (row + 1) * per], axis, offset)
        for row, axis, offset in ((0, "gx", 1), (1, "gx", -1), (2, "gy", 1), (3, "gy", -1))
    ]
    (moved,) = call(
        main_kernel, [((6, rows, LANES), F32)], sec, table, cell2, base,
        scratch=[dense] * 2, smem=(0,), busy_us=6,
    )
    pos_out, vel_out = call(
        settle_kernel, [(positions.shape, F32), (velocities.shape, F32)],
        left, low, mask, moved, *arrived,
        scratch=[pltpu.VMEM((6 * LANES, 4 * movers), BF16), pltpu.VMEM((6, rows, LANES), F32)],
        busy_us=4,
    )
    return p_out, v_out, pos_out, vel_out


def solution(mesh):
    placed = (
        P("gx", "gy", "sec"),
        P(None, "gx", "gy", "sec"),
        P(None, ("gx", "gy", "sec")),
        P(None, ("gx", "gy", "sec")),
        P(("gx", "gy", "sec")),
        P(("gx", "gy", "sec")),
        P(None, ("gx", "gy", "sec")),
        P(None, ("gx", "gy", "sec")),
    )
    return jax.shard_map(
        body,
        mesh=mesh,
        in_specs=placed,
        out_specs=(
            P("gx", "gy", "sec"),
            P(None, "gx", "gy", "sec"),
            P(None, ("gx", "gy", "sec")),
            P(None, ("gx", "gy", "sec")),
        ),
        check_vma=False,
    )
```

```python
import functools

import jax
import jax.numpy as jnp
from jax import lax
from jax.experimental import pallas as pl
from jax.experimental.pallas import tpu as pltpu
from jax.sharding import PartitionSpec as P

SWEEPS = 4
PAIRS = 8
BLOCK = 128
LANES = 128
HALO = SWEEPS + 1

TIME_STEP = 0.1
RELAX_RATE = 0.5
DAMPING = 0.5
RANGE_SQUARED = 16.0
GRAVITY = 1.0

F32 = jnp.float32
BF16 = jnp.bfloat16
NT = (((1,), (1,)), ((), ()))


def call(kernel, outs, *args, scratch=(), busy_us=0.1, smem=(), loose=()):
    outs_list = [jax.ShapeDtypeStruct(shape, dtype) for shape, dtype in outs]
    vmem = pl.BlockSpec(memory_space=pltpu.VMEM)
    scalar = pl.BlockSpec(memory_space=pltpu.SMEM)
    anywhere = pl.BlockSpec(memory_space=pl.ANY)
    specs = [scalar if i in smem else anywhere if i in loose else vmem for i in range(len(args))]
    return pl.pallas_call(
        kernel,
        out_shape=outs_list,
        in_specs=specs,
        out_specs=[vmem] * len(outs_list),
        scratch_shapes=list(scratch),
        compiler_params=pltpu.CompilerParams(vmem_limit_bytes=24 * 1024 * 1024),
        cost_estimate=pl.CostEstimate(flops=int(busy_us * 1.15e9), bytes_accessed=4096, transcendentals=0),
    )(*args)


def split(values):
    high = values.astype(BF16)
    return high, (values - high.astype(F32)).astype(BF16)


def row16(row):
    return jnp.broadcast_to(row, (16, row.shape[1])).astype(BF16)


def counters():
    base = lax.broadcasted_iota(jnp.int32, (16, LANES), 0)
    return [(base + 16 * k).astype(F32).astype(BF16) for k in range(8)]


def one_hot(row, counts, values=None):
    wide = row16(row)
    zero = jnp.zeros((16, LANES), BF16)
    if values is None:
        values = jnp.ones((16, LANES), BF16)
    return jnp.concatenate([jnp.where(wide == c, values, zero) for c in counts], axis=0)


def cell_split(cells, sec):
    high = (cells >> 8) + 64 * (((cells >> 7) & 1) ^ sec)
    return high, cells & (LANES - 1)


def ahead_kernel(out_ref):
    out_ref[...] = jnp.zeros(out_ref.shape, F32)


def deposit_kernel(sec_ref, vol_ref, cell_ref, after_ref, out_ref, hi_ref, lo_ref, va_ref, vb_ref):
    sec = sec_ref[0]
    high, low = cell_split(cell_ref[...], sec)
    hi_ref[...] = high.astype(F32)
    lo_ref[...] = low.astype(F32)
    vol = vol_ref[...]
    part = vol.astype(BF16).astype(F32)
    va_ref[...] = part
    vb_ref[...] = vol - part
    counts = counters()
    zero = jnp.zeros((16, LANES), BF16)
    rows_each = 16
    steps = vol_ref.shape[0] // rows_each

    def step(i, acc):
        lefts, rights = [], []
        for r in range(rows_each):
            at = pl.ds(i * rows_each + r, 1)
            lefts.append(one_hot(hi_ref[at, :], counts))
            low_row = row16(lo_ref[at, :])
            va, vb = row16(va_ref[at, :]), row16(vb_ref[at, :])
            hits = [low_row == c for c in counts]
            rights.append(
                jnp.concatenate(
                    [jnp.where(h, va, zero) for h in hits] + [jnp.where(h, vb, zero) for h in hits],
                    axis=0,
                )
            )
        left = jnp.concatenate(lefts, axis=1)
        right = jnp.concatenate(rights, axis=1)
        return acc + lax.dot_general(left, right, NT, preferred_element_type=F32)

    acc = lax.fori_loop(0, steps, step, jnp.zeros((LANES, 2 * LANES), F32), unroll=4)
    out_ref[...] = acc[:, :LANES] + acc[:, LANES:]


def contact_kernel(vol_ref, pos_ref, vel_ref, pair_ref, after_ref, base_ref):
    blocks = pos_ref.shape[1] // BLOCK
    base_ref[6] = RELAX_RATE * jnp.exp((-2.0 / 3.0) * jnp.log(vol_ref[...]))

    def step(b, carry):
        at = pl.ds(pl.multiple_of(b * BLOCK, BLOCK), BLOCK)
        index = pair_ref[:, at]
        mine = [pos_ref[d : d + 1, at] for d in range(3)] + [vel_ref[d : d + 1, at] for d in range(3)]
        wide = [jnp.broadcast_to(m, (PAIRS, BLOCK)) for m in mine]
        other = [jnp.take_along_axis(w, index, axis=1, mode="promise_in_bounds") for w in wide]
        apart = [wide[d] - other[d] for d in range(3)]
        dist = apart[0] * apart[0] + apart[1] * apart[1] + apart[2] * apart[2]
        weight = 1.0 / (1.0 + dist * (1.0 / RANGE_SQUARED))
        for d in range(3):
            push = weight * (apart[d] + DAMPING * (other[3 + d] - wide[3 + d]))
            force = jnp.sum(push, axis=0, keepdims=True)
            if d == 0:
                force = force - GRAVITY
            base_ref[d, pl.ds(b, 1), :] = mine[d]
            base_ref[3 + d, pl.ds(b, 1), :] = mine[3 + d] + TIME_STEP * force
        return carry

    lax.fori_loop(0, blocks, step, 0, unroll=32)


def table_of(fields, table_ref):
    for f, values in enumerate(fields):
        high, low = split(jnp.swapaxes(values, 0, 1))
        table_ref[f * LANES : (f + 1) * LANES, :LANES] = high
        table_ref[f * LANES : (f + 1) * LANES, LANES:] = low


def pick(table_ref, fields, high_rows, low_rows, counts):
    hot = jnp.concatenate([one_hot(row, counts) for row in high_rows], axis=1)
    hot = jnp.concatenate([hot, hot], axis=0)
    lane = lax.broadcasted_iota(jnp.int32, (LANES, LANES), 0).astype(F32)
    hits = [jnp.broadcast_to(row, (LANES, LANES)) == lane for row in low_rows]
    found = []
    for f in range(fields):
        rows = jnp.dot(table_ref[f * LANES : (f + 1) * LANES, :], hot, preferred_element_type=F32)
        found.append(
            [
                jnp.sum(jnp.where(hit, rows[:, LANES * h : LANES * (h + 1)], 0.0), axis=0, keepdims=True)
                for h, hit in enumerate(hits)
            ]
        )
    return found


def marks_kernel(dep_ref, after_ref, mask_ref, left_ref, low_ref):
    counts = counters()
    per = dep_ref.shape[1] // LANES
    for r in range(4):
        for q in range(per):
            row = dep_ref[r : r + 1, q * LANES : (q + 1) * LANES]
            hi_row, lane = (row >> 7).astype(F32), row & (LANES - 1)
            lanes = slice((r * per + q) * LANES, (r * per + q + 1) * LANES)
            for h in range(2):
                left_ref[h * LANES : (h + 1) * LANES, lanes] = one_hot(
                    jnp.where((lane >> 6) == h, hi_row, -1.0), counts
                )
            low_ref[:, lanes] = one_hot((lane & 63).astype(F32), counts[:4])
    mask_ref[...] = unfold(lax.dot_general(low_ref[...], left_ref[...], NT, preferred_element_type=F32))


def unfold(halves):
    return jnp.swapaxes(jnp.concatenate([halves[:, :LANES], halves[:, LANES:]], axis=0), 0, 1)


def leave_kernel(sec_ref, base_ref, cell_ref, dep_ref, after_ref, out_ref, hi_ref, lo_ref, table_ref):
    sec = sec_ref[0]
    high, low = cell_split(cell_ref[...], sec)
    cell = (high * LANES + low).astype(F32)
    table_of([base_ref[f] for f in range(7)] + [cell], table_ref)
    counts = counters()
    per = dep_ref.shape[1] // LANES
    for r in range(4):
        for q in range(per):
            row = dep_ref[r : r + 1, q * LANES : (q + 1) * LANES]
            k = r * per + q
            hi_ref[k : k + 1, :] = (row >> 7).astype(F32)
            lo_ref[k : k + 1, :] = (row & (LANES - 1)).astype(F32)

    def step(i, carry):
        ats = [pl.ds(2 * i + h, 1) for h in range(2)]
        found = pick(table_ref, 8, [hi_ref[at, :] for at in ats], [lo_ref[at, :] for at in ats], counts)
        for f in range(8):
            for h in range(2):
                out_ref[f, ats[h], :] = found[f][h]
        return carry

    lax.fori_loop(0, 2 * per, step, 0, unroll=16)


STATE = ((HALO, HALO, HALO), (HALO - 1, HALO, HALO), (HALO, HALO - 1, HALO), (HALO - 1, HALO - 1, HALO - 1))
VOID = ((HALO, HALO, HALO),)


def y_starts(spec):
    starts, at = [], 0
    for depth, _, _ in spec:
        for _ in range(2):
            starts.append(at)
            at += 8 * depth
    return starts, at


def x_starts(spec):
    starts, at = [], 0
    for _, depth, reach in spec:
        for _ in range(2):
            own = []
            for away in range(1, depth + 1):
                extra = min(HALO - 1, reach - away)
                own.append((at, extra))
                at += 8 + 2 * extra
            starts.append(own)
    return starts, at


def slices_y(spec, tile_ref, up_ref, down_ref):
    for g, start in enumerate(y_starts(spec)[0]):
        depth = spec[g // 2][0]
        for j in range(depth):
            at = start + 8 * j
            up_ref[at : at + 8, :] = tile_ref[g, pl.ds(8 - depth + j, 8, stride=8), :]
            down_ref[at : at + 8, :] = tile_ref[g, pl.ds(j, 8, stride=8), :]


def pack_kernel(p_ref, v_ref, after_ref, out_ref):
    out_ref[0:64, :] = p_ref[...]
    out_ref[64:256, :] = v_ref[...]


def early_kernel(near_ref, far_ref, tile_ref, up_ref, down_ref):
    for f in range(4):
        tile_ref[2 * f] = near_ref[64 * f : 64 * f + 64, :]
        tile_ref[2 * f + 1] = far_ref[64 * f : 64 * f + 64, :]
    slices_y(STATE, tile_ref, up_ref, down_ref)


def tile_kernel(mine_ref, got_ref, after_ref, tile_ref, up_ref, down_ref):
    own = mine_ref[0:64, :] + got_ref[64:128, :]
    far = mine_ref[64:128, :] + got_ref[0:64, :]
    tile_ref[0] = 1.0 / (1.0 + own)
    tile_ref[1] = 1.0 / (1.0 + far)
    slices_y(VOID, tile_ref, up_ref, down_ref)


def side_kernel(spec, tile_ref, low_ref, high_ref, after_ref, up_ref, down_ref):
    starts = x_starts(spec)[0]
    for g, y_start in enumerate(y_starts(spec)[0]):
        depth = spec[g // 2][0]
        for away, (start, extra) in enumerate(starts[g], 1):
            for x, out_ref in ((8 - away, up_ref), (away - 1, down_ref)):
                rows = [tile_ref[g, 8 * x : 8 * x + 8, :]]
                if extra > 0:
                    rows.insert(0, low_ref[pl.ds(y_start + 8 * (depth - extra) + x, extra, stride=8), :])
                    rows.append(high_ref[pl.ds(y_start + x, extra, stride=8), :])
                rows = jnp.concatenate(rows, axis=0) if extra > 0 else rows[0]
                out_ref[start : start + 8 + 2 * extra, :] = rows


def assemble(spec, tile_ref, ylow_ref, yhigh_ref, xlow_ref, xhigh_ref, grid_ref):
    filler = jnp.ones((8, LANES), F32)
    starts = x_starts(spec)[0]
    for g, y_start in enumerate(y_starts(spec)[0]):
        f, h = g // 2, g % 2
        depth = spec[f][0]
        lanes = slice(LANES * h, LANES * (h + 1))
        for x in list(range(HALO)) + list(range(HALO + 8, 2 * HALO + 8)):
            for m in range(3):
                grid_ref[f, x, 8 * m : 8 * m + 8, lanes] = filler
        for away, (start, extra) in enumerate(starts[g], 1):
            for x, side_ref in ((HALO - away, xlow_ref), (HALO + 7 + away, xhigh_ref)):
                grid_ref[f, x, 4 - extra : 12 + extra, lanes] = side_ref[start : start + 8 + 2 * extra, :]
        for x in range(8):
            far = depth - 4
            rows = [
                ylow_ref[pl.ds(y_start + 8 * far + x, 4, stride=8), :],
                tile_ref[g, 8 * x : 8 * x + 8, :],
                yhigh_ref[pl.ds(y_start + x, depth, stride=8), :],
                filler[: 8 - 2 * far],
            ]
            if far > 0:
                rows.append(ylow_ref[y_start + x : y_start + x + 1, :])
            grid_ref[f, HALO + x, 0:24, lanes] = jnp.concatenate(rows, axis=0)


def y_sides(values):
    return pltpu.roll(values, 23, 0), pltpu.roll(values, 1, 0)


def z_sides(values):
    return pltpu.roll(values, 2 * LANES - 1, 1), pltpu.roll(values, 1, 1)


def fluid_kernel(
    tile_ref, ylow_ref, yhigh_ref, xlow_ref, xhigh_ref, flow_ref, leave_ref,
    p_out_ref, v_out_ref, table_ref, sent_ref,
    void_ref, even_ref, odd_ref, invd_ref, div_ref, face_ref,
):
    size = 8 + 2 * HALO
    assemble(VOID, tile_ref, ylow_ref, yhigh_ref, xlow_ref, xhigh_ref, void_ref)

    for x in range(1, size - 1):
        void = void_ref[0, x]
        above, below = void_ref[0, x + 1], void_ref[0, x - 1]
        sides = y_sides(void) + z_sides(void)
        total = 6.0 * void + above + below
        for k in range(4):
            total = total + sides[k]
            face_ref[k, x] = void + sides[k]
        invd_ref[x] = 1.0 / total
        ys = y_sides(void * flow_ref[2, x])
        zs = z_sides(void * flow_ref[3, x])
        div_ref[x] = (
            above * flow_ref[1, x + 1] - below * flow_ref[1, x - 1] + (ys[0] - ys[1]) + (zs[0] - zs[1])
        )

    for t in range(SWEEPS):
        source = flow_ref.at[0] if t == 0 else even_ref if t % 2 == 0 else odd_ref
        target = odd_ref if t % 2 == 0 else even_ref
        for x in range(1 + t, size - 1 - t):
            void = void_ref[0, x]
            values = source[x]
            sides = y_sides(values) + z_sides(values)
            total = (void + void_ref[0, x + 1]) * source[x + 1] - div_ref[x]
            total = total + (void + void_ref[0, x - 1]) * source[x - 1]
            for k in range(4):
                total = total + face_ref[k, x] * sides[k]
            target[x] = total * invd_ref[x]

    final = even_ref if SWEEPS % 2 == 0 else odd_ref
    tables = [[], [], [], []]
    for x in range(8):
        values = final[HALO + x]
        ys, zs = y_sides(values), z_sides(values)
        flows = (
            flow_ref[1, HALO + x] - 0.5 * (final[HALO + x + 1] - final[HALO + x - 1]),
            flow_ref[2, HALO + x] - 0.5 * (ys[0] - ys[1]),
            flow_ref[3, HALO + x] - 0.5 * (zs[0] - zs[1]),
        )
        p_out_ref[x] = values[4:12, :LANES]
        tables[0].append(jnp.exp(-2.65 * jnp.log(void_ref[0, HALO + x][4:12])))
        for d in range(3):
            kept = flows[d][4:12]
            v_out_ref[d, x] = kept[:, :LANES]
            tables[1 + d].append(kept)
    fields = []
    for f in range(4):
        whole = jnp.concatenate(tables[f], axis=0)
        fields.append(jnp.concatenate([whole[:, :LANES], whole[:, LANES:]], axis=0))
    table_of(fields, table_ref)

    counts = counters()
    count = leave_ref.shape[1]

    def step(i, carry):
        his, los = [], []
        for h in range(2):
            cell = leave_ref[7, pl.ds(2 * i + h, 1), :].astype(jnp.int32)
            his.append((cell >> 7).astype(F32))
            los.append((cell & (LANES - 1)).astype(F32))
        found = pick(table_ref, 4, his, los, counts)
        for f in range(4):
            for h in range(2):
                sent_ref[f, pl.ds(2 * i + h, 1), :] = found[f][h]
        return carry

    lax.fori_loop(0, count // 2, step, 0, unroll=16)
    drag = TIME_STEP * sent_ref[0] * leave_ref[6]
    scale = 1.0 / (1.0 + drag)
    speeds = [(leave_ref[3 + d] + drag * sent_ref[1 + d]) * scale for d in range(3)]
    for d in range(3):
        sent_ref[3 + d] = speeds[d]
        sent_ref[d] = leave_ref[d] + TIME_STEP * speeds[d]


def flow_kernel(tile_ref, ylow_ref, yhigh_ref, xlow_ref, xhigh_ref, flow_ref):
    assemble(STATE, tile_ref, ylow_ref, yhigh_ref, xlow_ref, xhigh_ref, flow_ref)


def main_kernel(sec_ref, table_ref, cell_ref, base_ref, out_ref, hi_ref, lo_ref):
    sec = sec_ref[0]
    high, low = cell_split(cell_ref[...], sec)
    hi_ref[...] = high.astype(F32)
    lo_ref[...] = low.astype(F32)
    counts = counters()
    rows = cell_ref.shape[0]

    def step(i, carry):
        ats = [pl.ds(2 * i + h, 1) for h in range(2)]
        found = pick(table_ref, 4, [hi_ref[at, :] for at in ats], [lo_ref[at, :] for at in ats], counts)
        for f in range(4):
            for h in range(2):
                out_ref[f, ats[h], :] = found[f][h]
        return carry

    lax.fori_loop(0, rows // 2, step, 0, unroll=32)
    drag = TIME_STEP * out_ref[0] * base_ref[6]
    scale = 1.0 / (1.0 + drag)
    speeds = [(base_ref[3 + d] + drag * out_ref[1 + d]) * scale for d in range(3)]
    for d in range(3):
        out_ref[3 + d] = speeds[d]
        out_ref[d] = base_ref[d] + TIME_STEP * speeds[d]


def settle_kernel(
    left_ref, low_ref, mask_ref, moved_ref, a_ref, b_ref, c_ref, d_ref, pos_ref, vel_ref, right_ref, keep_ref,
):
    per = a_ref.shape[1]
    arrivals = (b_ref, a_ref, d_ref, c_ref)
    stays = mask_ref[...] < 0.5
    for f in range(6):
        for r in range(4):
            for q in range(per):
                value = arrivals[r][f, q : q + 1, :]
                part = value.astype(BF16).astype(F32)
                lanes = slice((r * per + q) * LANES, (r * per + q + 1) * LANES)
                for k, wide in enumerate((row16(part), row16(value - part))):
                    for m in range(4):
                        at = LANES * f + 64 * k + 16 * m
                        right_ref[at : at + 16, lanes] = low_ref[16 * m : 16 * m + 16, lanes] * wide
    placed = lax.dot_general(right_ref[...], left_ref[...], NT, preferred_element_type=F32)
    for f in range(6):
        rows = unfold(placed[LANES * f : LANES * f + 64] + placed[LANES * f + 64 : LANES * f + 128])
        keep_ref[f] = jnp.where(stays, moved_ref[f], rows)

    def spread(b, carry):
        at = pl.ds(pl.multiple_of(b * LANES, LANES), LANES)
        for d in range(3):
            pos_ref[d : d + 1, at] = keep_ref[d, pl.ds(b, 1), :]
            vel_ref[d : d + 1, at] = keep_ref[3 + d, pl.ds(b, 1), :]
        return carry

    lax.fori_loop(0, moved_ref.shape[1], spread, 0, unroll=16)


def shifted(block, axis, distance):
    count = lax.axis_size(axis)
    return lax.ppermute(block, axis, [((i - distance) % count, i) for i in range(count)])


def body(pressure, fluid_velocity, positions, velocities, volumes, cells, partners, departures):
    particles = volumes.shape[0]
    rows = particles // LANES
    movers = departures.shape[1]
    sec = lax.axis_index("sec").astype(jnp.int32).reshape(1)
    vol2 = volumes.reshape(rows, LANES)
    cell2 = cells.reshape(rows, LANES)
    near_p = pressure.reshape(64, LANES)
    near_v = fluid_velocity.reshape(192, LANES)
    dense = pltpu.VMEM((rows, LANES), F32)
    size = 8 + 2 * HALO
    leavers = 4 * movers // LANES

    (ahead,) = call(ahead_kernel, [((8, LANES), F32)], busy_us=3)
    (near,) = call(pack_kernel, [((256, LANES), F32)], near_p, near_v, ahead, loose=(2,), busy_us=3)
    far = shifted(near, "sec", 1)
    (mine,) = call(
        deposit_kernel, [((LANES, LANES), F32)], sec, vol2, cell2, near,
        scratch=[dense] * 4, smem=(0,), loose=(3,), busy_us=4,
    )
    got = shifted(mine, "sec", 1)
    state_y, state_x = y_starts(STATE)[1], x_starts(STATE)[1]
    void_y, void_x = y_starts(VOID)[1], x_starts(VOID)[1]
    state, state_up, state_down = call(
        early_kernel, [((8, 64, LANES), F32), ((state_y, LANES), F32), ((state_y, LANES), F32)],
        near, far,
    )
    state_ylow = shifted(state_up, "gy", 1)
    state_yhigh = shifted(state_down, "gy", -1)
    (base,) = call(
        contact_kernel, [((7, rows, LANES), F32)], vol2, positions, velocities, partners, state,
        loose=(4,), busy_us=4,
    )
    tile, up, down = call(
        tile_kernel, [((2, 64, LANES), F32), ((void_y, LANES), F32), ((void_y, LANES), F32)], mine, got, base,
        loose=(2,),
    )
    ylow = shifted(up, "gy", 1)
    yhigh = shifted(down, "gy", -1)
    state_xup, state_xdown = call(
        functools.partial(side_kernel, STATE), [((state_x, LANES), F32), ((state_x, LANES), F32)],
        state, state_ylow, state_yhigh, up, loose=(3,),
    )
    state_xlow = shifted(state_xup, "gx", 1)
    state_xhigh = shifted(state_xdown, "gx", -1)
    mask, left, low = call(
        marks_kernel, [((rows, LANES), F32), ((2 * LANES, 4 * movers), BF16), ((64, 4 * movers), BF16)],
        departures, state_xup, loose=(1,), busy_us=2,
    )
    xup, xdown = call(
        functools.partial(side_kernel, VOID), [((void_x, LANES), F32), ((void_x, LANES), F32)],
        tile, ylow, yhigh, mask, loose=(3,),
    )
    xlow = shifted(xup, "gx", 1)
    xhigh = shifted(xdown, "gx", -1)
    (leave,) = call(
        leave_kernel, [((8, leavers, LANES), F32)], sec, base, cell2, departures, xup,
        scratch=[
            pltpu.VMEM((leavers, LANES), F32), pltpu.VMEM((leavers, LANES), F32),
            pltpu.VMEM((8 * LANES, 2 * LANES), BF16),
        ],
        smem=(0,), loose=(4,), busy_us=3,
    )
    (flow,) = call(
        flow_kernel, [((4, size, 24, 2 * LANES), F32)], state, state_ylow, state_yhigh, state_xlow, state_xhigh, busy_us=1,
    )
    grid = pltpu.VMEM((size, 24, 2 * LANES), F32)
    p_out, v_out, table, sent = call(
        fluid_kernel,
        [
            (pressure.shape, F32), (fluid_velocity.shape, F32), ((4 * LANES, 2 * LANES), BF16),
            ((6, leavers, LANES), F32),
        ],
        tile, ylow, yhigh, xlow, xhigh, flow, leave,
        scratch=[
            pltpu.VMEM((1, size, 24, 2 * LANES), F32), grid, grid, grid, grid,
            pltpu.VMEM((4, size, 24, 2 * LANES), F32),
        ],
        busy_us=6,
    )
    per = movers // LANES
    arrived = [
        shifted(sent[:, row * per : (row + 1) * per], axis, offset)
        for row, axis, offset in ((0, "gx", 1), (1, "gx", -1), (2, "gy", 1), (3, "gy", -1))
    ]
    (moved,) = call(
        main_kernel, [((6, rows, LANES), F32)], sec, table, cell2, base,
        scratch=[dense] * 2, smem=(0,), busy_us=6,
    )
    pos_out, vel_out = call(
        settle_kernel, [(positions.shape, F32), (velocities.shape, F32)],
        left, low, mask, moved, *arrived,
        scratch=[pltpu.VMEM((6 * LANES, 4 * movers), BF16), pltpu.VMEM((6, rows, LANES), F32)],
        busy_us=4,
    )
    return p_out, v_out, pos_out, vel_out


def solution(mesh):
    placed = (
        P("gx", "gy", "sec"),
        P(None, "gx", "gy", "sec"),
        P(None, ("gx", "gy", "sec")),
        P(None, ("gx", "gy", "sec")),
        P(("gx", "gy", "sec")),
        P(("gx", "gy", "sec")),
        P(None, ("gx", "gy", "sec")),
        P(None, ("gx", "gy", "sec")),
    )
    return jax.shard_map(
        body,
        mesh=mesh,
        in_specs=placed,
        out_specs=(
            P("gx", "gy", "sec"),
            P(None, "gx", "gy", "sec"),
            P(None, ("gx", "gy", "sec")),
            P(None, ("gx", "gy", "sec")),
        ),
        check_vma=False,
    )
```

```python
import functools

import jax
import jax.numpy as jnp
from jax import lax
from jax.experimental import pallas as pl
from jax.experimental.pallas import tpu as pltpu
from jax.sharding import PartitionSpec as P

SWEEPS = 4
PAIRS = 8
BLOCK = 128
LANES = 128
HALO = SWEEPS + 1

TIME_STEP = 0.1
RELAX_RATE = 0.5
DAMPING = 0.5
RANGE_SQUARED = 16.0
GRAVITY = 1.0

F32 = jnp.float32
BF16 = jnp.bfloat16
NT = (((1,), (1,)), ((), ()))


def call(kernel, outs, *args, scratch=(), busy_us=0.1, smem=(), loose=()):
    outs_list = [jax.ShapeDtypeStruct(shape, dtype) for shape, dtype in outs]
    vmem = pl.BlockSpec(memory_space=pltpu.VMEM)
    scalar = pl.BlockSpec(memory_space=pltpu.SMEM)
    anywhere = pl.BlockSpec(memory_space=pl.ANY)
    specs = [scalar if i in smem else anywhere if i in loose else vmem for i in range(len(args))]
    return pl.pallas_call(
        kernel,
        out_shape=outs_list,
        in_specs=specs,
        out_specs=[vmem] * len(outs_list),
        scratch_shapes=list(scratch),
        compiler_params=pltpu.CompilerParams(vmem_limit_bytes=24 * 1024 * 1024),
        cost_estimate=pl.CostEstimate(flops=int(busy_us * 1.15e9), bytes_accessed=4096, transcendentals=0),
    )(*args)


def split(values):
    high = values.astype(BF16)
    return high, (values - high.astype(F32)).astype(BF16)


def row16(row):
    return jnp.broadcast_to(row, (16, row.shape[1])).astype(BF16)


def counters():
    base = lax.broadcasted_iota(jnp.int32, (16, LANES), 0)
    return [(base + 16 * k).astype(F32).astype(BF16) for k in range(8)]


def one_hot(row, counts, values=None):
    wide = row16(row)
    zero = jnp.zeros((16, LANES), BF16)
    if values is None:
        values = jnp.ones((16, LANES), BF16)
    return jnp.concatenate([jnp.where(wide == c, values, zero) for c in counts], axis=0)


def cell_split(cells, sec):
    high = (cells >> 8) + 64 * (((cells >> 7) & 1) ^ sec)
    return high, cells & (LANES - 1)


def ahead_kernel(out_ref):
    out_ref[...] = jnp.zeros(out_ref.shape, F32)


def deposit_kernel(sec_ref, vol_ref, cell_ref, after_ref, out_ref, hi_ref, lo_ref, va_ref, vb_ref):
    sec = sec_ref[0]
    high, low = cell_split(cell_ref[...], sec)
    hi_ref[...] = high.astype(F32)
    lo_ref[...] = low.astype(F32)
    vol = vol_ref[...]
    part = vol.astype(BF16).astype(F32)
    va_ref[...] = part
    vb_ref[...] = vol - part
    counts = counters()
    zero = jnp.zeros((16, LANES), BF16)
    rows_each = 16
    steps = vol_ref.shape[0] // rows_each

    def step(i, acc):
        lefts, rights = [], []
        for r in range(rows_each):
            at = pl.ds(i * rows_each + r, 1)
            lefts.append(one_hot(hi_ref[at, :], counts))
            low_row = row16(lo_ref[at, :])
            va, vb = row16(va_ref[at, :]), row16(vb_ref[at, :])
            hits = [low_row == c for c in counts]
            rights.append(
                jnp.concatenate(
                    [jnp.where(h, va, zero) for h in hits] + [jnp.where(h, vb, zero) for h in hits],
                    axis=0,
                )
            )
        left = jnp.concatenate(lefts, axis=1)
        right = jnp.concatenate(rights, axis=1)
        return acc + lax.dot_general(left, right, NT, preferred_element_type=F32)

    acc = lax.fori_loop(0, steps, step, jnp.zeros((LANES, 2 * LANES), F32), unroll=8)
    out_ref[...] = acc[:, :LANES] + acc[:, LANES:]


def contact_kernel(vol_ref, pos_ref, vel_ref, pair_ref, after_ref, base_ref):
    blocks = pos_ref.shape[1] // BLOCK
    base_ref[6] = RELAX_RATE * jnp.exp((-2.0 / 3.0) * jnp.log(vol_ref[...]))

    def step(b, carry):
        at = pl.ds(pl.multiple_of(b * BLOCK, BLOCK), BLOCK)
        index = pair_ref[:, at]
        mine = [pos_ref[d : d + 1, at] for d in range(3)] + [vel_ref[d : d + 1, at] for d in range(3)]
        wide = [jnp.broadcast_to(m, (PAIRS, BLOCK)) for m in mine]
        other = [jnp.take_along_axis(w, index, axis=1, mode="promise_in_bounds") for w in wide]
        apart = [wide[d] - other[d] for d in range(3)]
        dist = apart[0] * apart[0] + apart[1] * apart[1] + apart[2] * apart[2]
        weight = 1.0 / (1.0 + dist * (1.0 / RANGE_SQUARED))
        for d in range(3):
            push = weight * (apart[d] + DAMPING * (other[3 + d] - wide[3 + d]))
            force = jnp.sum(push, axis=0, keepdims=True)
            if d == 0:
                force = force - GRAVITY
            base_ref[d, pl.ds(b, 1), :] = mine[d]
            base_ref[3 + d, pl.ds(b, 1), :] = mine[3 + d] + TIME_STEP * force
        return carry

    lax.fori_loop(0, blocks, step, 0, unroll=64)


def table_of(fields, table_ref):
    for f, values in enumerate(fields):
        high, low = split(jnp.swapaxes(values, 0, 1))
        table_ref[f * LANES : (f + 1) * LANES, :LANES] = high
        table_ref[f * LANES : (f + 1) * LANES, LANES:] = low


def pick(table_ref, fields, high_rows, low_rows, counts):
    hot = jnp.concatenate([one_hot(row, counts) for row in high_rows], axis=1)
    hot = jnp.concatenate([hot, hot], axis=0)
    lane = lax.broadcasted_iota(jnp.int32, (LANES, LANES), 0).astype(F32)
    hits = [jnp.broadcast_to(row, (LANES, LANES)) == lane for row in low_rows]
    found = []
    for f in range(fields):
        rows = jnp.dot(table_ref[f * LANES : (f + 1) * LANES, :], hot, preferred_element_type=F32)
        found.append(
            [
                jnp.sum(jnp.where(hit, rows[:, LANES * h : LANES * (h + 1)], 0.0), axis=0, keepdims=True)
                for h, hit in enumerate(hits)
            ]
        )
    return found


def marks_kernel(dep_ref, after_ref, mask_ref, left_ref, low_ref):
    counts = counters()
    per = dep_ref.shape[1] // LANES
    for r in range(4):
        for q in range(per):
            row = dep_ref[r : r + 1, q * LANES : (q + 1) * LANES]
            hi_row, lane = (row >> 7).astype(F32), row & (LANES - 1)
            lanes = slice((r * per + q) * LANES, (r * per + q + 1) * LANES)
            for h in range(2):
                left_ref[h * LANES : (h + 1) * LANES, lanes] = one_hot(
                    jnp.where((lane >> 6) == h, hi_row, -1.0), counts
                )
            low_ref[:, lanes] = one_hot((lane & 63).astype(F32), counts[:4])
    mask_ref[...] = unfold(lax.dot_general(low_ref[...], left_ref[...], NT, preferred_element_type=F32))


def unfold(halves):
    return jnp.swapaxes(jnp.concatenate([halves[:, :LANES], halves[:, LANES:]], axis=0), 0, 1)


def leave_kernel(sec_ref, base_ref, cell_ref, dep_ref, after_ref, out_ref, hi_ref, lo_ref, table_ref):
    sec = sec_ref[0]
    high, low = cell_split(cell_ref[...], sec)
    cell = (high * LANES + low).astype(F32)
    table_of([base_ref[f] for f in range(7)] + [cell], table_ref)
    counts = counters()
    per = dep_ref.shape[1] // LANES
    for r in range(4):
        for q in range(per):
            row = dep_ref[r : r + 1, q * LANES : (q + 1) * LANES]
            k = r * per + q
            hi_ref[k : k + 1, :] = (row >> 7).astype(F32)
            lo_ref[k : k + 1, :] = (row & (LANES - 1)).astype(F32)

    def step(i, carry):
        ats = [pl.ds(2 * i + h, 1) for h in range(2)]
        found = pick(table_ref, 8, [hi_ref[at, :] for at in ats], [lo_ref[at, :] for at in ats], counts)
        for f in range(8):
            for h in range(2):
                out_ref[f, ats[h], :] = found[f][h]
        return carry

    lax.fori_loop(0, 2 * per, step, 0, unroll=16)


STATE = ((HALO - 1, HALO, HALO), (HALO, HALO - 1, HALO), (HALO - 1, HALO - 1, HALO - 1))
VOID = ((HALO, HALO, HALO), (HALO, HALO, HALO))


def y_starts(spec):
    starts, at = [], 0
    for depth, _, _ in spec:
        for _ in range(2):
            starts.append(at)
            at += 8 * depth
    return starts, at


def x_starts(spec):
    starts, at = [], 0
    for _, depth, reach in spec:
        for _ in range(2):
            own = []
            for away in range(1, depth + 1):
                extra = min(HALO - 1, reach - away)
                own.append((at, extra))
                at += 8 + 2 * extra
            starts.append(own)
    return starts, at


def slices_y(spec, tile_ref, up_ref, down_ref):
    for g, start in enumerate(y_starts(spec)[0]):
        depth = spec[g // 2][0]
        for j in range(depth):
            at = start + 8 * j
            up_ref[at : at + 8, :] = tile_ref[g, pl.ds(8 - depth + j, 8, stride=8), :]
            down_ref[at : at + 8, :] = tile_ref[g, pl.ds(j, 8, stride=8), :]


def pack_kernel(p_ref, v_ref, after_ref, out_ref):
    out_ref[0:64, :] = p_ref[...]
    out_ref[64:256, :] = v_ref[...]


def early_kernel(near_ref, far_ref, tile_ref, up_ref, down_ref):
    for d in range(3):
        tile_ref[2 * d] = near_ref[64 * d + 64 : 64 * d + 128, :]
        tile_ref[2 * d + 1] = far_ref[64 * d + 64 : 64 * d + 128, :]
    slices_y(STATE, tile_ref, up_ref, down_ref)


def tile_kernel(mine_ref, got_ref, near_ref, far_ref, after_ref, tile_ref, up_ref, down_ref):
    own = mine_ref[0:64, :] + got_ref[64:128, :]
    far = mine_ref[64:128, :] + got_ref[0:64, :]
    tile_ref[0] = 1.0 / (1.0 + own)
    tile_ref[1] = 1.0 / (1.0 + far)
    tile_ref[2] = near_ref[0:64, :]
    tile_ref[3] = far_ref[0:64, :]
    slices_y(VOID, tile_ref, up_ref, down_ref)


def side_kernel(spec, tile_ref, low_ref, high_ref, after_ref, up_ref, down_ref):
    starts = x_starts(spec)[0]
    for g, y_start in enumerate(y_starts(spec)[0]):
        depth = spec[g // 2][0]
        for away, (start, extra) in enumerate(starts[g], 1):
            for x, out_ref in ((8 - away, up_ref), (away - 1, down_ref)):
                rows = [tile_ref[g, 8 * x : 8 * x + 8, :]]
                if extra > 0:
                    rows.insert(0, low_ref[pl.ds(y_start + 8 * (depth - extra) + x, extra, stride=8), :])
                    rows.append(high_ref[pl.ds(y_start + x, extra, stride=8), :])
                rows = jnp.concatenate(rows, axis=0) if extra > 0 else rows[0]
                out_ref[start : start + 8 + 2 * extra, :] = rows


def assemble(spec, tile_ref, ylow_ref, yhigh_ref, xlow_ref, xhigh_ref, grid_ref):
    filler = jnp.ones((8, LANES), F32)
    starts = x_starts(spec)[0]
    for g, y_start in enumerate(y_starts(spec)[0]):
        f, h = g // 2, g % 2
        depth = spec[f][0]
        lanes = slice(LANES * h, LANES * (h + 1))
        for x in list(range(HALO)) + list(range(HALO + 8, 2 * HALO + 8)):
            for m in range(3):
                grid_ref[f, x, 8 * m : 8 * m + 8, lanes] = filler
        for away, (start, extra) in enumerate(starts[g], 1):
            for x, side_ref in ((HALO - away, xlow_ref), (HALO + 7 + away, xhigh_ref)):
                grid_ref[f, x, 4 - extra : 12 + extra, lanes] = side_ref[start : start + 8 + 2 * extra, :]
        for x in range(8):
            far = depth - 4
            rows = [
                ylow_ref[pl.ds(y_start + 8 * far + x, 4, stride=8), :],
                tile_ref[g, 8 * x : 8 * x + 8, :],
                yhigh_ref[pl.ds(y_start + x, depth, stride=8), :],
                filler[: 8 - 2 * far],
            ]
            if far > 0:
                rows.append(ylow_ref[y_start + x : y_start + x + 1, :])
            grid_ref[f, HALO + x, 0:24, lanes] = jnp.concatenate(rows, axis=0)


def y_sides(values):
    return pltpu.roll(values, 23, 0), pltpu.roll(values, 1, 0)


def z_sides(values):
    return pltpu.roll(values, 2 * LANES - 1, 1), pltpu.roll(values, 1, 1)


def fluid_kernel(
    tile_ref, ylow_ref, yhigh_ref, xlow_ref, xhigh_ref, flow_ref, leave_ref,
    p_out_ref, v_out_ref, table_ref, sent_ref,
    void_ref, even_ref, odd_ref, invd_ref, div_ref, face_ref,
):
    size = 8 + 2 * HALO
    assemble(VOID, tile_ref, ylow_ref, yhigh_ref, xlow_ref, xhigh_ref, void_ref)

    for x in range(1, size - 1):
        void = void_ref[0, x]
        above, below = void_ref[0, x + 1], void_ref[0, x - 1]
        sides = y_sides(void) + z_sides(void)
        total = 6.0 * void + above + below
        for k in range(4):
            total = total + sides[k]
            face_ref[k, x] = void + sides[k]
        invd_ref[x] = 1.0 / total
        ys = y_sides(void * flow_ref[1, x])
        zs = z_sides(void * flow_ref[2, x])
        div_ref[x] = (
            above * flow_ref[0, x + 1] - below * flow_ref[0, x - 1] + (ys[0] - ys[1]) + (zs[0] - zs[1])
        )

    for t in range(SWEEPS):
        source = void_ref.at[1] if t == 0 else even_ref if t % 2 == 0 else odd_ref
        target = odd_ref if t % 2 == 0 else even_ref
        for x in range(1 + t, size - 1 - t):
            void = void_ref[0, x]
            values = source[x]
            sides = y_sides(values) + z_sides(values)
            total = (void + void_ref[0, x + 1]) * source[x + 1] - div_ref[x]
            total = total + (void + void_ref[0, x - 1]) * source[x - 1]
            for k in range(4):
                total = total + face_ref[k, x] * sides[k]
            target[x] = total * invd_ref[x]

    final = even_ref if SWEEPS % 2 == 0 else odd_ref
    tables = [[], [], [], []]
    for x in range(8):
        values = final[HALO + x]
        ys, zs = y_sides(values), z_sides(values)
        flows = (
            flow_ref[0, HALO + x] - 0.5 * (final[HALO + x + 1] - final[HALO + x - 1]),
            flow_ref[1, HALO + x] - 0.5 * (ys[0] - ys[1]),
            flow_ref[2, HALO + x] - 0.5 * (zs[0] - zs[1]),
        )
        p_out_ref[x] = values[4:12, :LANES]
        tables[0].append(jnp.exp(-2.65 * jnp.log(void_ref[0, HALO + x][4:12])))
        for d in range(3):
            kept = flows[d][4:12]
            v_out_ref[d, x] = kept[:, :LANES]
            tables[1 + d].append(kept)
    fields = []
    for f in range(4):
        whole = jnp.concatenate(tables[f], axis=0)
        fields.append(jnp.concatenate([whole[:, :LANES], whole[:, LANES:]], axis=0))
    table_of(fields, table_ref)

    counts = counters()
    count = leave_ref.shape[1]

    def step(i, carry):
        his, los = [], []
        for h in range(2):
            cell = leave_ref[7, pl.ds(2 * i + h, 1), :].astype(jnp.int32)
            his.append((cell >> 7).astype(F32))
            los.append((cell & (LANES - 1)).astype(F32))
        found = pick(table_ref, 4, his, los, counts)
        for f in range(4):
            for h in range(2):
                sent_ref[f, pl.ds(2 * i + h, 1), :] = found[f][h]
        return carry

    lax.fori_loop(0, count // 2, step, 0, unroll=16)
    drag = TIME_STEP * sent_ref[0] * leave_ref[6]
    scale = 1.0 / (1.0 + drag)
    speeds = [(leave_ref[3 + d] + drag * sent_ref[1 + d]) * scale for d in range(3)]
    for d in range(3):
        sent_ref[3 + d] = speeds[d]
        sent_ref[d] = leave_ref[d] + TIME_STEP * speeds[d]


def flow_kernel(tile_ref, ylow_ref, yhigh_ref, xlow_ref, xhigh_ref, flow_ref):
    assemble(STATE, tile_ref, ylow_ref, yhigh_ref, xlow_ref, xhigh_ref, flow_ref)


def main_kernel(sec_ref, table_ref, cell_ref, base_ref, out_ref, hi_ref, lo_ref):
    sec = sec_ref[0]
    high, low = cell_split(cell_ref[...], sec)
    hi_ref[...] = high.astype(F32)
    lo_ref[...] = low.astype(F32)
    counts = counters()
    rows = cell_ref.shape[0]

    def step(i, carry):
        ats = [pl.ds(2 * i + h, 1) for h in range(2)]
        found = pick(table_ref, 4, [hi_ref[at, :] for at in ats], [lo_ref[at, :] for at in ats], counts)
        for f in range(4):
            for h in range(2):
                out_ref[f, ats[h], :] = found[f][h]
        return carry

    lax.fori_loop(0, rows // 2, step, 0, unroll=64)
    drag = TIME_STEP * out_ref[0] * base_ref[6]
    scale = 1.0 / (1.0 + drag)
    speeds = [(base_ref[3 + d] + drag * out_ref[1 + d]) * scale for d in range(3)]
    for d in range(3):
        out_ref[3 + d] = speeds[d]
        out_ref[d] = base_ref[d] + TIME_STEP * speeds[d]


def settle_kernel(
    left_ref, low_ref, mask_ref, moved_ref, a_ref, b_ref, c_ref, d_ref, pos_ref, vel_ref, right_ref, keep_ref,
):
    per = a_ref.shape[1]
    arrivals = (b_ref, a_ref, d_ref, c_ref)
    stays = mask_ref[...] < 0.5
    for f in range(6):
        for r in range(4):
            for q in range(per):
                value = arrivals[r][f, q : q + 1, :]
                part = value.astype(BF16).astype(F32)
                lanes = slice((r * per + q) * LANES, (r * per + q + 1) * LANES)
                for k, wide in enumerate((row16(part), row16(value - part))):
                    for m in range(4):
                        at = LANES * f + 64 * k + 16 * m
                        right_ref[at : at + 16, lanes] = low_ref[16 * m : 16 * m + 16, lanes] * wide
    placed = lax.dot_general(right_ref[...], left_ref[...], NT, preferred_element_type=F32)
    for f in range(6):
        rows = unfold(placed[LANES * f : LANES * f + 64] + placed[LANES * f + 64 : LANES * f + 128])
        keep_ref[f] = jnp.where(stays, moved_ref[f], rows)

    def spread(b, carry):
        at = pl.ds(pl.multiple_of(b * LANES, LANES), LANES)
        for d in range(3):
            pos_ref[d : d + 1, at] = keep_ref[d, pl.ds(b, 1), :]
            vel_ref[d : d + 1, at] = keep_ref[3 + d, pl.ds(b, 1), :]
        return carry

    lax.fori_loop(0, moved_ref.shape[1], spread, 0, unroll=64)


def shifted(block, axis, distance):
    count = lax.axis_size(axis)
    return lax.ppermute(block, axis, [((i - distance) % count, i) for i in range(count)])


def body(pressure, fluid_velocity, positions, velocities, volumes, cells, partners, departures):
    particles = volumes.shape[0]
    rows = particles // LANES
    movers = departures.shape[1]
    sec = lax.axis_index("sec").astype(jnp.int32).reshape(1)
    vol2 = volumes.reshape(rows, LANES)
    cell2 = cells.reshape(rows, LANES)
    near_p = pressure.reshape(64, LANES)
    near_v = fluid_velocity.reshape(192, LANES)
    dense = pltpu.VMEM((rows, LANES), F32)
    size = 8 + 2 * HALO
    leavers = 4 * movers // LANES

    (ahead,) = call(ahead_kernel, [((8, LANES), F32)], busy_us=3)
    (near,) = call(pack_kernel, [((256, LANES), F32)], near_p, near_v, ahead, loose=(2,), busy_us=3)
    far = shifted(near, "sec", 1)
    (mine,) = call(
        deposit_kernel, [((LANES, LANES), F32)], sec, vol2, cell2, near,
        scratch=[dense] * 4, smem=(0,), loose=(3,), busy_us=4,
    )
    got = shifted(mine, "sec", 1)
    state_y, state_x = y_starts(STATE)[1], x_starts(STATE)[1]
    void_y, void_x = y_starts(VOID)[1], x_starts(VOID)[1]
    state, state_up, state_down = call(
        early_kernel, [((6, 64, LANES), F32), ((state_y, LANES), F32), ((state_y, LANES), F32)],
        near, far,
    )
    state_ylow = shifted(state_up, "gy", 1)
    state_yhigh = shifted(state_down, "gy", -1)
    (base,) = call(
        contact_kernel, [((7, rows, LANES), F32)], vol2, positions, velocities, partners, state,
        loose=(4,), busy_us=4,
    )
    tile, up, down = call(
        tile_kernel, [((4, 64, LANES), F32), ((void_y, LANES), F32), ((void_y, LANES), F32)], mine, got, near, far, base,
        loose=(4,),
    )
    ylow = shifted(up, "gy", 1)
    yhigh = shifted(down, "gy", -1)
    state_xup, state_xdown = call(
        functools.partial(side_kernel, STATE), [((state_x, LANES), F32), ((state_x, LANES), F32)],
        state, state_ylow, state_yhigh, up, loose=(3,),
    )
    state_xlow = shifted(state_xup, "gx", 1)
    state_xhigh = shifted(state_xdown, "gx", -1)
    mask, left, low = call(
        marks_kernel, [((rows, LANES), F32), ((2 * LANES, 4 * movers), BF16), ((64, 4 * movers), BF16)],
        departures, state_xup, loose=(1,), busy_us=2,
    )
    xup, xdown = call(
        functools.partial(side_kernel, VOID), [((void_x, LANES), F32), ((void_x, LANES), F32)],
        tile, ylow, yhigh, mask, loose=(3,),
    )
    xlow = shifted(xup, "gx", 1)
    xhigh = shifted(xdown, "gx", -1)
    (leave,) = call(
        leave_kernel, [((8, leavers, LANES), F32)], sec, base, cell2, departures, xup,
        scratch=[
            pltpu.VMEM((leavers, LANES), F32), pltpu.VMEM((leavers, LANES), F32),
            pltpu.VMEM((8 * LANES, 2 * LANES), BF16),
        ],
        smem=(0,), loose=(4,), busy_us=3,
    )
    (flow,) = call(
        flow_kernel, [((3, size, 24, 2 * LANES), F32)], state, state_ylow, state_yhigh, state_xlow, state_xhigh, busy_us=1,
    )
    grid = pltpu.VMEM((size, 24, 2 * LANES), F32)
    p_out, v_out, table, sent = call(
        fluid_kernel,
        [
            (pressure.shape, F32), (fluid_velocity.shape, F32), ((4 * LANES, 2 * LANES), BF16),
            ((6, leavers, LANES), F32),
        ],
        tile, ylow, yhigh, xlow, xhigh, flow, leave,
        scratch=[
            pltpu.VMEM((2, size, 24, 2 * LANES), F32), grid, grid, grid, grid,
            pltpu.VMEM((4, size, 24, 2 * LANES), F32),
        ],
        busy_us=6,
    )
    per = movers // LANES
    arrived = [
        shifted(sent[:, row * per : (row + 1) * per], axis, offset)
        for row, axis, offset in ((0, "gx", 1), (1, "gx", -1), (2, "gy", 1), (3, "gy", -1))
    ]
    (moved,) = call(
        main_kernel, [((6, rows, LANES), F32)], sec, table, cell2, base,
        scratch=[dense] * 2, smem=(0,), busy_us=6,
    )
    pos_out, vel_out = call(
        settle_kernel, [(positions.shape, F32), (velocities.shape, F32)],
        left, low, mask, moved, *arrived,
        scratch=[pltpu.VMEM((6 * LANES, 4 * movers), BF16), pltpu.VMEM((6, rows, LANES), F32)],
        busy_us=4,
    )
    return p_out, v_out, pos_out, vel_out


def solution(mesh):
    placed = (
        P("gx", "gy", "sec"),
        P(None, "gx", "gy", "sec"),
        P(None, ("gx", "gy", "sec")),
        P(None, ("gx", "gy", "sec")),
        P(("gx", "gy", "sec")),
        P(("gx", "gy", "sec")),
        P(None, ("gx", "gy", "sec")),
        P(None, ("gx", "gy", "sec")),
    )
    return jax.shard_map(
        body,
        mesh=mesh,
        in_specs=placed,
        out_specs=(
            P("gx", "gy", "sec"),
            P(None, "gx", "gy", "sec"),
            P(None, ("gx", "gy", "sec")),
            P(None, ("gx", "gy", "sec")),
        ),
        check_vma=False,
    )
```

```python
import functools

import jax
import jax.numpy as jnp
from jax import lax
from jax.experimental import pallas as pl
from jax.experimental.pallas import tpu as pltpu
from jax.sharding import PartitionSpec as P

SWEEPS = 4
PAIRS = 8
BLOCK = 128
LANES = 128
HALO = SWEEPS + 1

TIME_STEP = 0.1
RELAX_RATE = 0.5
DAMPING = 0.5
RANGE_SQUARED = 16.0
GRAVITY = 1.0

F32 = jnp.float32
BF16 = jnp.bfloat16
NT = (((1,), (1,)), ((), ()))


def call(kernel, outs, *args, scratch=(), busy_us=0.1, smem=(), loose=()):
    outs_list = [jax.ShapeDtypeStruct(shape, dtype) for shape, dtype in outs]
    vmem = pl.BlockSpec(memory_space=pltpu.VMEM)
    scalar = pl.BlockSpec(memory_space=pltpu.SMEM)
    anywhere = pl.BlockSpec(memory_space=pl.ANY)
    specs = [scalar if i in smem else anywhere if i in loose else vmem for i in range(len(args))]
    return pl.pallas_call(
        kernel,
        out_shape=outs_list,
        in_specs=specs,
        out_specs=[vmem] * len(outs_list),
        scratch_shapes=list(scratch),
        compiler_params=pltpu.CompilerParams(vmem_limit_bytes=24 * 1024 * 1024),
        cost_estimate=pl.CostEstimate(flops=int(busy_us * 1.15e9), bytes_accessed=4096, transcendentals=0),
    )(*args)


def split(values):
    high = values.astype(BF16)
    return high, (values - high.astype(F32)).astype(BF16)


def row16(row):
    return jnp.broadcast_to(row, (16, row.shape[1])).astype(BF16)


def counters():
    base = lax.broadcasted_iota(jnp.int32, (16, LANES), 0)
    return [(base + 16 * k).astype(F32).astype(BF16) for k in range(8)]


def one_hot(row, counts, values=None):
    wide = row16(row)
    zero = jnp.zeros((16, LANES), BF16)
    if values is None:
        values = jnp.ones((16, LANES), BF16)
    return jnp.concatenate([jnp.where(wide == c, values, zero) for c in counts], axis=0)


def cell_split(cells, sec):
    high = (cells >> 8) + 64 * (((cells >> 7) & 1) ^ sec)
    return high, cells & (LANES - 1)


def ahead_kernel(out_ref):
    out_ref[...] = jnp.zeros(out_ref.shape, F32)


def deposit_kernel(sec_ref, vol_ref, cell_ref, after_ref, out_ref, hi_ref, lo_ref, va_ref, vb_ref):
    sec = sec_ref[0]
    high, low = cell_split(cell_ref[...], sec)
    hi_ref[...] = high.astype(F32)
    lo_ref[...] = low.astype(F32)
    vol = vol_ref[...]
    part = vol.astype(BF16).astype(F32)
    va_ref[...] = part
    vb_ref[...] = vol - part
    counts = counters()
    zero = jnp.zeros((16, LANES), BF16)
    rows_each = 16
    steps = vol_ref.shape[0] // rows_each

    def step(i, acc):
        lefts, rights = [], []
        for r in range(rows_each):
            at = pl.ds(i * rows_each + r, 1)
            lefts.append(one_hot(hi_ref[at, :], counts))
            low_row = row16(lo_ref[at, :])
            va, vb = row16(va_ref[at, :]), row16(vb_ref[at, :])
            hits = [low_row == c for c in counts]
            rights.append(
                jnp.concatenate(
                    [jnp.where(h, va, zero) for h in hits] + [jnp.where(h, vb, zero) for h in hits],
                    axis=0,
                )
            )
        left = jnp.concatenate(lefts, axis=1)
        right = jnp.concatenate(rights, axis=1)
        return acc + lax.dot_general(left, right, NT, preferred_element_type=F32)

    acc = lax.fori_loop(0, steps, step, jnp.zeros((LANES, 2 * LANES), F32), unroll=8)
    out_ref[...] = acc[:, :LANES] + acc[:, LANES:]


def contact_kernel(vol_ref, pos_ref, vel_ref, pair_ref, after_ref, base_ref):
    blocks = pos_ref.shape[1] // BLOCK
    base_ref[6] = RELAX_RATE * jnp.exp((-2.0 / 3.0) * jnp.log(vol_ref[...]))

    def step(b, carry):
        at = pl.ds(pl.multiple_of(b * BLOCK, BLOCK), BLOCK)
        index = pair_ref[:, at]
        mine = [pos_ref[d : d + 1, at] for d in range(3)] + [vel_ref[d : d + 1, at] for d in range(3)]
        wide = [jnp.broadcast_to(m, (PAIRS, BLOCK)) for m in mine]
        other = [jnp.take_along_axis(w, index, axis=1, mode="promise_in_bounds") for w in wide]
        apart = [wide[d] - other[d] for d in range(3)]
        dist = apart[0] * apart[0] + apart[1] * apart[1] + apart[2] * apart[2]
        weight = 1.0 / (1.0 + dist * (1.0 / RANGE_SQUARED))
        for d in range(3):
            push = weight * (apart[d] + DAMPING * (other[3 + d] - wide[3 + d]))
            force = jnp.sum(push, axis=0, keepdims=True)
            if d == 0:
                force = force - GRAVITY
            base_ref[d, pl.ds(b, 1), :] = mine[d]
            base_ref[3 + d, pl.ds(b, 1), :] = mine[3 + d] + TIME_STEP * force
        return carry

    lax.fori_loop(0, blocks, step, 0, unroll=64)


def table_of(fields, table_ref):
    for f, values in enumerate(fields):
        high, low = split(jnp.swapaxes(values, 0, 1))
        table_ref[f * LANES : (f + 1) * LANES, :LANES] = high
        table_ref[f * LANES : (f + 1) * LANES, LANES:] = low


def pick(table_ref, fields, high_rows, low_rows, counts):
    hot = jnp.concatenate([one_hot(row, counts) for row in high_rows], axis=1)
    hot = jnp.concatenate([hot, hot], axis=0)
    lane = lax.broadcasted_iota(jnp.int32, (LANES, LANES), 0).astype(F32)
    hits = [jnp.broadcast_to(row, (LANES, LANES)) == lane for row in low_rows]
    found = []
    for f in range(fields):
        rows = jnp.dot(table_ref[f * LANES : (f + 1) * LANES, :], hot, preferred_element_type=F32)
        found.append(
            [
                jnp.sum(jnp.where(hit, rows[:, LANES * h : LANES * (h + 1)], 0.0), axis=0, keepdims=True)
                for h, hit in enumerate(hits)
            ]
        )
    return found


def marks_kernel(dep_ref, after_ref, mask_ref, left_ref, low_ref):
    counts = counters()
    per = dep_ref.shape[1] // LANES
    for r in range(4):
        for q in range(per):
            row = dep_ref[r : r + 1, q * LANES : (q + 1) * LANES]
            hi_row, lane = (row >> 7).astype(F32), row & (LANES - 1)
            lanes = slice((r * per + q) * LANES, (r * per + q + 1) * LANES)
            for h in range(2):
                left_ref[h * LANES : (h + 1) * LANES, lanes] = one_hot(
                    jnp.where((lane >> 6) == h, hi_row, -1.0), counts
                )
            low_ref[:, lanes] = one_hot((lane & 63).astype(F32), counts[:4])
    mask_ref[...] = unfold(lax.dot_general(low_ref[...], left_ref[...], NT, preferred_element_type=F32))


def unfold(halves):
    return jnp.swapaxes(jnp.concatenate([halves[:, :LANES], halves[:, LANES:]], axis=0), 0, 1)


def leave_kernel(sec_ref, base_ref, cell_ref, dep_ref, after_ref, out_ref, hi_ref, lo_ref, table_ref):
    sec = sec_ref[0]
    high, low = cell_split(cell_ref[...], sec)
    cell = (high * LANES + low).astype(F32)
    table_of([base_ref[f] for f in range(7)] + [cell], table_ref)
    counts = counters()
    per = dep_ref.shape[1] // LANES
    for r in range(4):
        for q in range(per):
            row = dep_ref[r : r + 1, q * LANES : (q + 1) * LANES]
            k = r * per + q
            hi_ref[k : k + 1, :] = (row >> 7).astype(F32)
            lo_ref[k : k + 1, :] = (row & (LANES - 1)).astype(F32)

    def step(i, carry):
        ats = [pl.ds(2 * i + h, 1) for h in range(2)]
        found = pick(table_ref, 8, [hi_ref[at, :] for at in ats], [lo_ref[at, :] for at in ats], counts)
        for f in range(8):
            for h in range(2):
                out_ref[f, ats[h], :] = found[f][h]
        return carry

    lax.fori_loop(0, 2 * per, step, 0, unroll=16)


STATE = ((HALO - 1, HALO, HALO), (HALO, HALO - 1, HALO), (HALO - 1, HALO - 1, HALO - 1))
VOID = ((HALO, HALO, HALO), (HALO, HALO, HALO))


def y_starts(spec):
    starts, at = [], 0
    for depth, _, _ in spec:
        for _ in range(2):
            starts.append(at)
            at += 8 * depth
    return starts, at


def x_starts(spec):
    starts, at = [], 0
    for _, depth, reach in spec:
        for _ in range(2):
            own = []
            for away in range(1, depth + 1):
                extra = min(HALO - 1, reach - away)
                own.append((at, extra))
                at += 8 + 2 * extra
            starts.append(own)
    return starts, at


def slices_y(spec, tile_ref, up_ref, down_ref):
    for g, start in enumerate(y_starts(spec)[0]):
        depth = spec[g // 2][0]
        for j in range(depth):
            at = start + 8 * j
            up_ref[at : at + 8, :] = tile_ref[g, pl.ds(8 - depth + j, 8, stride=8), :]
            down_ref[at : at + 8, :] = tile_ref[g, pl.ds(j, 8, stride=8), :]


def pack_kernel(p_ref, v_ref, after_ref, out_ref):
    out_ref[0:64, :] = p_ref[...]
    out_ref[64:256, :] = v_ref[...]


def early_kernel(near_ref, far_ref, tile_ref, up_ref, down_ref):
    for d in range(3):
        tile_ref[2 * d] = near_ref[64 * d + 64 : 64 * d + 128, :]
        tile_ref[2 * d + 1] = far_ref[64 * d + 64 : 64 * d + 128, :]
    slices_y(STATE, tile_ref, up_ref, down_ref)


def tile_kernel(mine_ref, got_ref, near_ref, far_ref, after_ref, tile_ref, up_ref, down_ref):
    own = mine_ref[0:64, :] + got_ref[64:128, :]
    far = mine_ref[64:128, :] + got_ref[0:64, :]
    tile_ref[0] = 1.0 / (1.0 + own)
    tile_ref[1] = 1.0 / (1.0 + far)
    tile_ref[2] = near_ref[0:64, :]
    tile_ref[3] = far_ref[0:64, :]
    slices_y(VOID, tile_ref, up_ref, down_ref)


def side_kernel(spec, tile_ref, low_ref, high_ref, after_ref, up_ref, down_ref):
    starts = x_starts(spec)[0]
    for g, y_start in enumerate(y_starts(spec)[0]):
        depth = spec[g // 2][0]
        for away, (start, extra) in enumerate(starts[g], 1):
            for x, out_ref in ((8 - away, up_ref), (away - 1, down_ref)):
                rows = [tile_ref[g, 8 * x : 8 * x + 8, :]]
                if extra > 0:
                    rows.insert(0, low_ref[pl.ds(y_start + 8 * (depth - extra) + x, extra, stride=8), :])
                    rows.append(high_ref[pl.ds(y_start + x, extra, stride=8), :])
                rows = jnp.concatenate(rows, axis=0) if extra > 0 else rows[0]
                out_ref[start : start + 8 + 2 * extra, :] = rows


def assemble_sides(spec, xlow_ref, xhigh_ref, grid_ref):
    filler = jnp.ones((8, LANES), F32)
    starts = x_starts(spec)[0]
    for g in range(2 * len(spec)):
        f, h = g // 2, g % 2
        lanes = slice(LANES * h, LANES * (h + 1))
        for x in list(range(HALO)) + list(range(HALO + 8, 2 * HALO + 8)):
            for m in range(3):
                grid_ref[f, x, 8 * m : 8 * m + 8, lanes] = filler
        for away, (start, extra) in enumerate(starts[g], 1):
            for x, side_ref in ((HALO - away, xlow_ref), (HALO + 7 + away, xhigh_ref)):
                grid_ref[f, x, 4 - extra : 12 + extra, lanes] = side_ref[start : start + 8 + 2 * extra, :]


def assemble_middle(spec, tile_ref, ylow_ref, yhigh_ref, grid_ref, first):
    filler = jnp.ones((8, LANES), F32)
    for g, y_start in enumerate(y_starts(spec)[0]):
        f, h = g // 2, g % 2
        depth = spec[f][0]
        lanes = slice(LANES * h, LANES * (h + 1))
        for x in range(8):
            far = depth - 4
            rows = [
                ylow_ref[pl.ds(y_start + 8 * far + x, 4, stride=8), :],
                tile_ref[g, 8 * x : 8 * x + 8, :],
                yhigh_ref[pl.ds(y_start + x, depth, stride=8), :],
                filler[: 8 - 2 * far],
            ]
            if far > 0:
                rows.append(ylow_ref[y_start + x : y_start + x + 1, :])
            grid_ref[f, first + x, 0:24, lanes] = jnp.concatenate(rows, axis=0)


def y_sides(values):
    return pltpu.roll(values, 23, 0), pltpu.roll(values, 1, 0)


def z_sides(values):
    return pltpu.roll(values, 2 * LANES - 1, 1), pltpu.roll(values, 1, 1)


def set_up(void, flow_ref, x):
    middle, above, below = void(x), void(x + 1), void(x - 1)
    sides = y_sides(middle) + z_sides(middle)
    total = 6.0 * middle + above + below
    for k in range(4):
        total = total + sides[k]
    ys = y_sides(middle * flow_ref[1, x])
    zs = z_sides(middle * flow_ref[2, x])
    source = above * flow_ref[0, x + 1] - below * flow_ref[0, x - 1] + (ys[0] - ys[1]) + (zs[0] - zs[1])
    return [middle + side for side in sides], 1.0 / total, source


def swept(void, press, faces, inverse, source, x):
    values = press(x)
    sides = y_sides(values) + z_sides(values)
    total = (void(x) + void(x + 1)) * press(x + 1) - source
    total = total + (void(x) + void(x - 1)) * press(x - 1)
    for k in range(4):
        total = total + faces[k] * sides[k]
    return total * inverse


FIRST, LAST = HALO + 1, HALO + 7


def fluid_kernel(
    xlow_ref, xhigh_ref, flow_ref, own_ref, inner_ref, leave_ref,
    p_out_ref, v_out_ref, table_ref, sent_ref,
    void_ref, even_ref, odd_ref, set_ref,
):
    size = 8 + 2 * HALO
    assemble_sides(VOID, xlow_ref, xhigh_ref, void_ref)

    def field(f):
        return lambda x: own_ref[f, x - HALO] if HALO <= x < HALO + 8 else void_ref[f, x]

    void = field(0)

    def setting(k, x):
        return inner_ref[k, x - FIRST] if FIRST <= x < LAST else set_ref[k, x]

    for x in range(1, size - 1):
        if not FIRST <= x < LAST:
            faces, inverse, source = set_up(void, flow_ref, x)
            for k, values in enumerate(faces + [inverse, source]):
                set_ref[k, x] = values

    def first_sweep(x):
        return inner_ref[6, x - FIRST] if FIRST <= x < LAST else odd_ref[x]

    for t in range(SWEEPS):
        before = field(1) if t == 0 else first_sweep if t == 1 else (lambda x, ref=even_ref if t % 2 == 0 else odd_ref: ref[x])
        target = odd_ref if t % 2 == 0 else even_ref
        for x in range(1 + t, size - 1 - t):
            if t > 0 or not FIRST <= x < LAST:
                faces = [setting(k, x) for k in range(4)]
                target[x] = swept(void, before, faces, setting(4, x), setting(5, x), x)

    final = even_ref if SWEEPS % 2 == 0 else odd_ref
    tables = [[], [], [], []]
    for x in range(8):
        values = final[HALO + x]
        ys, zs = y_sides(values), z_sides(values)
        flows = (
            flow_ref[0, HALO + x] - 0.5 * (final[HALO + x + 1] - final[HALO + x - 1]),
            flow_ref[1, HALO + x] - 0.5 * (ys[0] - ys[1]),
            flow_ref[2, HALO + x] - 0.5 * (zs[0] - zs[1]),
        )
        p_out_ref[x] = values[4:12, :LANES]
        tables[0].append(jnp.exp(-2.65 * jnp.log(own_ref[0, x][4:12])))
        for d in range(3):
            kept = flows[d][4:12]
            v_out_ref[d, x] = kept[:, :LANES]
            tables[1 + d].append(kept)
    fields = []
    for f in range(4):
        whole = jnp.concatenate(tables[f], axis=0)
        fields.append(jnp.concatenate([whole[:, :LANES], whole[:, LANES:]], axis=0))
    table_of(fields, table_ref)

    counts = counters()
    count = leave_ref.shape[1]

    def step(i, carry):
        his, los = [], []
        for h in range(2):
            cell = leave_ref[7, pl.ds(2 * i + h, 1), :].astype(jnp.int32)
            his.append((cell >> 7).astype(F32))
            los.append((cell & (LANES - 1)).astype(F32))
        found = pick(table_ref, 4, his, los, counts)
        for f in range(4):
            for h in range(2):
                sent_ref[f, pl.ds(2 * i + h, 1), :] = found[f][h]
        return carry

    lax.fori_loop(0, count // 2, step, 0, unroll=16)
    drag = TIME_STEP * sent_ref[0] * leave_ref[6]
    scale = 1.0 / (1.0 + drag)
    speeds = [(leave_ref[3 + d] + drag * sent_ref[1 + d]) * scale for d in range(3)]
    for d in range(3):
        sent_ref[3 + d] = speeds[d]
        sent_ref[d] = leave_ref[d] + TIME_STEP * speeds[d]


def flow_kernel(
    tile_ref, ylow_ref, yhigh_ref, xlow_ref, xhigh_ref, void_tile_ref, void_low_ref, void_high_ref,
    flow_ref, own_ref, inner_ref,
):
    assemble_sides(STATE, xlow_ref, xhigh_ref, flow_ref)
    assemble_middle(STATE, tile_ref, ylow_ref, yhigh_ref, flow_ref, HALO)
    assemble_middle(VOID, void_tile_ref, void_low_ref, void_high_ref, own_ref, 0)
    void, press = (lambda x: own_ref[0, x - HALO]), (lambda x: own_ref[1, x - HALO])
    for x in range(FIRST, LAST):
        faces, inverse, source = set_up(void, flow_ref, x)
        result = swept(void, press, faces, inverse, source, x)
        for k, values in enumerate(faces + [inverse, source, result]):
            inner_ref[k, x - FIRST] = values


def main_kernel(sec_ref, table_ref, cell_ref, base_ref, out_ref, hi_ref, lo_ref):
    sec = sec_ref[0]
    high, low = cell_split(cell_ref[...], sec)
    hi_ref[...] = high.astype(F32)
    lo_ref[...] = low.astype(F32)
    counts = counters()
    rows = cell_ref.shape[0]

    def step(i, carry):
        ats = [pl.ds(2 * i + h, 1) for h in range(2)]
        found = pick(table_ref, 4, [hi_ref[at, :] for at in ats], [lo_ref[at, :] for at in ats], counts)
        for f in range(4):
            for h in range(2):
                out_ref[f, ats[h], :] = found[f][h]
        return carry

    lax.fori_loop(0, rows // 2, step, 0, unroll=64)
    drag = TIME_STEP * out_ref[0] * base_ref[6]
    scale = 1.0 / (1.0 + drag)
    speeds = [(base_ref[3 + d] + drag * out_ref[1 + d]) * scale for d in range(3)]
    for d in range(3):
        out_ref[3 + d] = speeds[d]
        out_ref[d] = base_ref[d] + TIME_STEP * speeds[d]


def settle_kernel(
    left_ref, low_ref, mask_ref, moved_ref, a_ref, b_ref, c_ref, d_ref, pos_ref, vel_ref, right_ref, keep_ref,
):
    per = a_ref.shape[1]
    arrivals = (b_ref, a_ref, d_ref, c_ref)
    stays = mask_ref[...] < 0.5
    for f in range(6):
        for r in range(4):
            for q in range(per):
                value = arrivals[r][f, q : q + 1, :]
                part = value.astype(BF16).astype(F32)
                lanes = slice((r * per + q) * LANES, (r * per + q + 1) * LANES)
                for k, wide in enumerate((row16(part), row16(value - part))):
                    for m in range(4):
                        at = LANES * f + 64 * k + 16 * m
                        right_ref[at : at + 16, lanes] = low_ref[16 * m : 16 * m + 16, lanes] * wide
    placed = lax.dot_general(right_ref[...], left_ref[...], NT, preferred_element_type=F32)
    for f in range(6):
        rows = unfold(placed[LANES * f : LANES * f + 64] + placed[LANES * f + 64 : LANES * f + 128])
        keep_ref[f] = jnp.where(stays, moved_ref[f], rows)

    def spread(b, carry):
        at = pl.ds(pl.multiple_of(b * LANES, LANES), LANES)
        for d in range(3):
            pos_ref[d : d + 1, at] = keep_ref[d, pl.ds(b, 1), :]
            vel_ref[d : d + 1, at] = keep_ref[3 + d, pl.ds(b, 1), :]
        return carry

    lax.fori_loop(0, moved_ref.shape[1], spread, 0, unroll=64)


def shifted(block, axis, distance):
    count = lax.axis_size(axis)
    return lax.ppermute(block, axis, [((i - distance) % count, i) for i in range(count)])


def body(pressure, fluid_velocity, positions, velocities, volumes, cells, partners, departures):
    particles = volumes.shape[0]
    rows = particles // LANES
    movers = departures.shape[1]
    sec = lax.axis_index("sec").astype(jnp.int32).reshape(1)
    vol2 = volumes.reshape(rows, LANES)
    cell2 = cells.reshape(rows, LANES)
    near_p = pressure.reshape(64, LANES)
    near_v = fluid_velocity.reshape(192, LANES)
    dense = pltpu.VMEM((rows, LANES), F32)
    size = 8 + 2 * HALO
    leavers = 4 * movers // LANES

    (ahead,) = call(ahead_kernel, [((8, LANES), F32)], busy_us=3)
    (near,) = call(pack_kernel, [((256, LANES), F32)], near_p, near_v, ahead, loose=(2,), busy_us=3)
    far = shifted(near, "sec", 1)
    (mine,) = call(
        deposit_kernel, [((LANES, LANES), F32)], sec, vol2, cell2, near,
        scratch=[dense] * 4, smem=(0,), loose=(3,), busy_us=4,
    )
    got = shifted(mine, "sec", 1)
    state_y, state_x = y_starts(STATE)[1], x_starts(STATE)[1]
    void_y, void_x = y_starts(VOID)[1], x_starts(VOID)[1]
    state, state_up, state_down = call(
        early_kernel, [((6, 64, LANES), F32), ((state_y, LANES), F32), ((state_y, LANES), F32)],
        near, far,
    )
    state_ylow = shifted(state_up, "gy", 1)
    state_yhigh = shifted(state_down, "gy", -1)
    (base,) = call(
        contact_kernel, [((7, rows, LANES), F32)], vol2, positions, velocities, partners, state,
        loose=(4,), busy_us=4,
    )
    tile, up, down = call(
        tile_kernel, [((4, 64, LANES), F32), ((void_y, LANES), F32), ((void_y, LANES), F32)], mine, got, near, far, base,
        loose=(4,),
    )
    ylow = shifted(up, "gy", 1)
    yhigh = shifted(down, "gy", -1)
    state_xup, state_xdown = call(
        functools.partial(side_kernel, STATE), [((state_x, LANES), F32), ((state_x, LANES), F32)],
        state, state_ylow, state_yhigh, up, loose=(3,),
    )
    state_xlow = shifted(state_xup, "gx", 1)
    state_xhigh = shifted(state_xdown, "gx", -1)
    mask, left, low = call(
        marks_kernel, [((rows, LANES), F32), ((2 * LANES, 4 * movers), BF16), ((64, 4 * movers), BF16)],
        departures, state_xup, loose=(1,), busy_us=2,
    )
    xup, xdown = call(
        functools.partial(side_kernel, VOID), [((void_x, LANES), F32), ((void_x, LANES), F32)],
        tile, ylow, yhigh, mask, loose=(3,),
    )
    xlow = shifted(xup, "gx", 1)
    xhigh = shifted(xdown, "gx", -1)
    (leave,) = call(
        leave_kernel, [((8, leavers, LANES), F32)], sec, base, cell2, departures, xup,
        scratch=[
            pltpu.VMEM((leavers, LANES), F32), pltpu.VMEM((leavers, LANES), F32),
            pltpu.VMEM((8 * LANES, 2 * LANES), BF16),
        ],
        smem=(0,), loose=(4,), busy_us=3,
    )
    flow, own, inner = call(
        flow_kernel,
        [
            ((3, size, 24, 2 * LANES), F32), ((2, 8, 24, 2 * LANES), F32), ((7, LAST - FIRST, 24, 2 * LANES), F32),
        ],
        state, state_ylow, state_yhigh, state_xlow, state_xhigh, tile, ylow, yhigh, busy_us=1,
    )
    grid = pltpu.VMEM((size, 24, 2 * LANES), F32)
    p_out, v_out, table, sent = call(
        fluid_kernel,
        [
            (pressure.shape, F32), (fluid_velocity.shape, F32), ((4 * LANES, 2 * LANES), BF16),
            ((6, leavers, LANES), F32),
        ],
        xlow, xhigh, flow, own, inner, leave,
        scratch=[
            pltpu.VMEM((2, size, 24, 2 * LANES), F32), grid, grid, pltpu.VMEM((6, size, 24, 2 * LANES), F32),
        ],
        busy_us=6,
    )
    per = movers // LANES
    arrived = [
        shifted(sent[:, row * per : (row + 1) * per], axis, offset)
        for row, axis, offset in ((0, "gx", 1), (1, "gx", -1), (2, "gy", 1), (3, "gy", -1))
    ]
    (moved,) = call(
        main_kernel, [((6, rows, LANES), F32)], sec, table, cell2, base,
        scratch=[dense] * 2, smem=(0,), busy_us=6,
    )
    pos_out, vel_out = call(
        settle_kernel, [(positions.shape, F32), (velocities.shape, F32)],
        left, low, mask, moved, *arrived,
        scratch=[pltpu.VMEM((6 * LANES, 4 * movers), BF16), pltpu.VMEM((6, rows, LANES), F32)],
        busy_us=4,
    )
    return p_out, v_out, pos_out, vel_out


def solution(mesh):
    placed = (
        P("gx", "gy", "sec"),
        P(None, "gx", "gy", "sec"),
        P(None, ("gx", "gy", "sec")),
        P(None, ("gx", "gy", "sec")),
        P(("gx", "gy", "sec")),
        P(("gx", "gy", "sec")),
        P(None, ("gx", "gy", "sec")),
        P(None, ("gx", "gy", "sec")),
    )
    return jax.shard_map(
        body,
        mesh=mesh,
        in_specs=placed,
        out_specs=(
            P("gx", "gy", "sec"),
            P(None, "gx", "gy", "sec"),
            P(None, ("gx", "gy", "sec")),
            P(None, ("gx", "gy", "sec")),
        ),
        check_vma=False,
    )
```
